512 devices in a mesh: wide: 64 (over z, x, core), narrow: 8 (over y).
Axes of the slice: x: 4, y: 8, z: 8, core: 2. Of those that a mesh axis runs over, the one named last changes fastest.
Arguments:
- weight: bfloat16 [8192, 53248], P('narrow', 'wide'), may hold values from -0.0625 to 0.0625
- whitening: bfloat16 [8192, 8192], P('wide', 'narrow'), as said below
- sketch: bfloat16 [53248, 256], P('wide'), may hold values from -6 to 6
Outputs:
- basis: float32 [8192, 256], P(('wide', 'narrow'))
- projected: float32 [256, 53248], P('narrow', 'wide')
The draws below stay inside these ranges and needn't reach their ends.
Inputs may be any that keep to these rules, and one draw needn't show every extreme that they name: `whitening`: zero below the diagonal; diagonal entries between 0.7 and 1.4.
All inputs are finite; a program needn't handle non-finite values.
Results may differ from the reference program's by a relative error of at most 0.02.
Values may be sent and summed in bfloat16 or wider, within the bound.
A program may use at most 64 MiB of HBM per device.

```python
import math
import jax
import jax.numpy as jnp
from jax import lax

D = 8192
F = 53248
R = 256


def draw_whitening(key, part):
    key = jax.random.fold_in(key, 7)
    key_off, key_diag = jax.random.split(key)
    row_index = lax.broadcasted_iota(jnp.int32, (D, D), 0)
    col_index = lax.broadcasted_iota(jnp.int32, (D, D), 1)
    offdiag = jax.random.normal(key_off, (D, D), jnp.float32) * (1.5 / math.sqrt(D))
    diagonal = jax.random.uniform(key_diag, (D, D), jnp.float32, 0.7, 1.4)
    upper = jnp.where(col_index > row_index, offdiag, jnp.where(col_index == row_index, diagonal, 0.0))
    return upper.astype(jnp.bfloat16)


def shard_levels(stream_key, shape, shards, least, high):
    def one(dim, shards_of):
        heights = jax.random.uniform(jax.random.fold_in(jax.random.fold_in(stream_key, 6), dim), (shards_of,), jnp.float32, least / len(shards), high / len(shards))
        return jnp.repeat(jnp.exp(heights), shape[dim] // shards_of).reshape((-1,) + (1,) * (len(shape) - dim - 1))

    level = one(*shards[0])
    for cut in shards[1:]:
        level = level * one(*cut)
    return level


def bell_draw(rng, extent, width, reach, cuts=(), dtype=jnp.bfloat16):
    drawn = width * jax.random.normal(rng, extent, jnp.float32)
    if cuts:
        drawn = drawn * shard_levels(rng, extent, cuts, -0.22, 0.18)
    return jnp.clip(drawn, -reach, reach).astype(dtype)


def setup_inputs(seed: int = 0) -> dict:
    key_of = jax.random.split(jax.random.key(seed), 4)
    weight = bell_draw(key_of[0], (D, F), D ** -0.5, 0.0625, ((0, 8), (1, 64)))
    whitening = draw_whitening(jax.random.fold_in(key_of[3], 71), 0)
    sketch = bell_draw(key_of[2], (F, R), 1.0, 6.0, ((0, 64),))
    return dict(weight=weight, whitening=whitening, sketch=sketch)


def reference(weight, whitening, sketch):
    sketch_image = jnp.dot(weight.astype(jnp.float32), sketch.astype(jnp.float32), preferred_element_type=jnp.float32).astype(jnp.bfloat16)
    whitened = jnp.dot(whitening.astype(jnp.float32), sketch_image.astype(jnp.float32), preferred_element_type=jnp.float32).astype(jnp.bfloat16)
    back_image = jnp.dot(whitening.T.astype(jnp.float32), whitened.astype(jnp.float32), preferred_element_type=jnp.float32).astype(jnp.bfloat16)
    feature_image = jnp.dot(weight.T.astype(jnp.float32), back_image.astype(jnp.float32), preferred_element_type=jnp.float32).astype(jnp.bfloat16)
    second_image = jnp.dot(weight.astype(jnp.float32), feature_image.astype(jnp.float32), preferred_element_type=jnp.float32).astype(jnp.bfloat16)
    final_rows = jnp.dot(whitening.astype(jnp.float32), second_image.astype(jnp.float32), preferred_element_type=jnp.float32)
    gram_matrix = jnp.dot(final_rows.T, final_rows, precision=lax.Precision.HIGHEST)
    lower_factor = jnp.linalg.cholesky(gram_matrix)
    basis_full = jax.scipy.linalg.solve_triangular(lower_factor, final_rows.T, lower=True).T
    basis = basis_full * jnp.float32(math.sqrt(D))
    basis_low = basis_full.astype(jnp.bfloat16)
    weighted = jnp.dot(whitening.T.astype(jnp.float32), basis_low.astype(jnp.float32), preferred_element_type=jnp.float32).astype(jnp.bfloat16)
    projected = jnp.dot(weighted.T.astype(jnp.float32), weight.astype(jnp.float32), preferred_element_type=jnp.float32)
    return (basis, projected)
```

```python
import math

import jax
import jax.numpy as jnp
from jax import lax
from jax.experimental import pallas as pl
from jax.experimental.pallas import tpu as pltpu
from jax.sharding import PartitionSpec as P

D = 8192
R = 256
NX, NZ, NY = 4, 8, 8
BF = jnp.bfloat16
F32 = jnp.float32
MESH = pl.DeviceIdType.MESH


def ds(start, size):
    if isinstance(start, int):
        return pl.ds(start, size)
    return pl.ds(pl.multiple_of(start, size), size)


class Rows:
    full, half, xc, zc, dtype = (1024, 256), (512, 256), (128, 256), (16, 256), BF

    @staticmethod
    def x_of(q):
        return (ds(q * 128, 128), slice(None))

    @staticmethod
    def z_of(q):
        return (ds(q * 16, 16), slice(None))

    @staticmethod
    def f_x(c, x):
        return (ds(c * 512 + x * 128, 128), slice(None))

    @staticmethod
    def f_z(c, x, z):
        return (ds(c * 512 + x * 128 + z * 16, 16), slice(None))


class Cols:
    full, half, xc, zc, dtype = (256, 1024), (128, 1024), (32, 1024), (32, 128), BF

    @staticmethod
    def x_of(q):
        return (ds(q * 32, 32), slice(None))

    @staticmethod
    def z_of(q):
        return (slice(None), ds(q * 128, 128))

    @staticmethod
    def f_x(c, x):
        return (ds(c * 128 + x * 32, 32), slice(None))

    @staticmethod
    def f_z(c, x, z):
        return (ds(c * 128 + x * 32, 32), ds(z * 128, 128))


class Gram:
    full, half, xc, zc, dtype = (256, 256), (128, 256), (32, 256), (8, 128), F32

    @staticmethod
    def x_of(q):
        return (ds(q * 32, 32), slice(None))

    @staticmethod
    def z_of(q):
        return (ds((q // 2) * 8, 8), ds((q % 2) * 128, 128))

    @staticmethod
    def f_x(c, x):
        return (ds(c * 128 + x * 32, 32), slice(None))

    @staticmethod
    def f_z(c, x, z):
        return (ds(c * 128 + x * 32 + (z // 2) * 8, 8), ds((z % 2) * 128, 128))


WIDE = (Rows, Cols, Rows, Gram, Cols)
NARROW = (((128, 256), 16), ((256, 832), 32), ((128, 256), 16), ((256, 832), 32))


def wide_scratch(lay):
    vm = pltpu.VMEM
    return [
        vm(lay.half, F32),
        vm(lay.half, lay.dtype),
        vm(lay.half, lay.dtype),
        vm((3,) + lay.xc, lay.dtype),
        vm((3,) + lay.xc, lay.dtype),
        vm(lay.xc, F32),
        vm(lay.xc, lay.dtype),
        vm((7,) + lay.zc, lay.dtype),
        vm(lay.full, lay.dtype),
        pltpu.SemaphoreType.DMA((14,)),
        pltpu.SemaphoreType.DMA((14,)),
    ]


def narrow_scratch(spec):
    shape, rows = spec
    return [
        pltpu.VMEM(shape, BF),
        pltpu.VMEM((rows, shape[1]), F32),
        pltpu.VMEM((7, rows, shape[1]), BF),
        pltpu.VMEM(shape, BF),
        pltpu.SemaphoreType.DMA((2,)),
        pltpu.SemaphoreType.DMA((2,)),
    ]


def dot(a, b):
    return jnp.dot(a, b, preferred_element_type=F32)


def dot_exact(a, b):
    return jnp.dot(a, b, preferred_element_type=F32, precision=lax.Precision.HIGHEST)


class Place:
    def __init__(self):
        w = lax.axis_index("wide")
        self.n = lax.axis_index("narrow")
        self.core = w % 2
        self.x = (w // 2) % NX
        self.z = w // (2 * NX)

    def wide(self, z, x, core):
        return {"wide": (z * NX + x) * 2 + core}

    @property
    def sibling(self):
        return self.wide(self.z, self.x, 1 - self.core)

    def x_peer(self, k):
        return self.wide(self.z, (self.x + k) % NX, self.core)

    def z_peer(self, k):
        return self.wide((self.z + k) % NZ, self.x, self.core)

    def y_peer(self, k):
        return {"narrow": (self.n + k) % NY}


def send(src, dst, ssem, rsem, where):
    copy = pltpu.make_async_remote_copy(
        src_ref=src, dst_ref=dst, send_sem=ssem, recv_sem=rsem, device_id=where, device_id_type=MESH
    )
    copy.start()


def wait_bytes(ref, sem):
    pltpu.make_async_copy(ref, ref, sem).wait()


class WideSum:
    def __init__(self, lay, here, bufs):
        self.lay, self.here = lay, here
        (self.keep, self.csend, self.crecv, self.xsend, self.xrecv, self.own,
         self.zsend, self.zrecv, self.full, self.ss, self.rs) = bufs

    def start(self, make_half, after_first=None):
        lay, here = self.lay, self.here
        self.csend[...] = make_half(1 - here.core).astype(lay.dtype)
        if after_first is not None:
            after_first()
        for k in (2, 1, 3, 0):
            q = lay.x_of((here.x + k) % NX)
            send(self.csend.at[q], self.crecv.at[q], self.ss.at[k], self.rs.at[k], here.sibling)
        self.keep[...] = make_half(here.core)

    def x_step(self):
        lay, here = self.lay, self.here
        for k in (2, 1, 3, 0):
            q = lay.x_of((here.x + k) % NX)
            wait_bytes(self.crecv.at[q], self.rs.at[k])
            total = self.keep[q] + self.crecv[q].astype(F32)
            if k:
                self.xsend[k - 1] = total.astype(lay.dtype)
                send(self.xsend.at[k - 1], self.xrecv.at[k - 1], self.ss.at[4], self.rs.at[4], here.x_peer(k))
            else:
                self.own[...] = total

    def z_step(self):
        lay, here = self.lay, self.here
        wait_bytes(self.xrecv, self.rs.at[4])
        total = self.own[...]
        for k in range(3):
            total = total + self.xrecv[k].astype(F32)
        self.own[...] = total
        self.zsend[...] = total.astype(lay.dtype)
        for k in (4, 3, 5, 2, 6, 1, 7):
            send(self.zsend.at[lay.z_of((here.z + k) % NZ)], self.zrecv.at[k - 1],
                 self.ss.at[5], self.rs.at[5], here.z_peer(k))

    def z_back(self):
        lay, here = self.lay, self.here
        wait_bytes(self.zrecv, self.rs.at[5])
        total = self.own[lay.z_of(here.z)]
        for k in range(7):
            total = total + self.zrecv[k].astype(F32)
        mine = lay.f_z(here.core, here.x, here.z)
        self.full[mine] = total.astype(lay.dtype)
        for k in (4, 3, 5, 2, 6, 1, 7):
            send(self.full.at[mine], self.full.at[mine], self.ss.at[6], self.rs.at[6], here.z_peer(k))

    def x_back(self):
        lay, here = self.lay, self.here
        wait_bytes(self.zrecv, self.rs.at[6])
        mine = lay.f_x(here.core, here.x)
        for k in (2, 1, 3):
            send(self.full.at[mine], self.full.at[mine], self.ss.at[6 + k], self.rs.at[6 + k], here.x_peer(k))
        send(self.full.at[mine], self.full.at[mine], self.ss.at[10], self.rs.at[10], here.sibling)

    def core_back(self):
        lay, here = self.lay, self.here
        for k in (1, 3, 2):
            there = lay.f_x(here.core, (here.x + NX - k) % NX)
            wait_bytes(self.full.at[there], self.rs.at[6 + k])
            send(self.full.at[there], self.full.at[there], self.ss.at[10 + k], self.rs.at[10 + k], here.sibling)

    def finish(self):
        lay, here = self.lay, self.here
        for k in (0, 1, 3, 2):
            there = lay.f_x(1 - here.core, (here.x + NX - k) % NX)
            wait_bytes(self.full.at[there], self.rs.at[10 + k])

    def drain(self):
        lay, here = self.lay, self.here
        for k in range(4):
            wait_bytes(self.csend.at[lay.x_of(k)], self.ss.at[k])
        wait_bytes(self.xsend, self.ss.at[4])
        for j in (5, 6):
            wait_bytes(self.zrecv, self.ss.at[j])
        for j in range(7, 14):
            wait_bytes(self.full.at[lay.f_x(0, 0)], self.ss.at[j])

    def gather(self):
        self.x_step()
        self.z_step()
        self.z_back()
        self.x_back()
        self.core_back()
        self.finish()
        return self.full


class NarrowSum:
    def __init__(self, spec, here, bufs):
        self.rows, self.here = spec[1], here
        self.sendbuf, self.own, self.recv, self.full, self.ss, self.rs = bufs
        self.gathers = False

    def scatter(self, total):
        rows, here = self.rows, self.here
        self.sendbuf[...] = total.astype(BF)
        for k in (4, 3, 5, 2, 6, 1, 7):
            send(self.sendbuf.at[ds(((here.n + k) % NY) * rows, rows)], self.recv.at[k - 1],
                 self.ss.at[0], self.rs.at[0], here.y_peer(k))
        mine = self.sendbuf[ds(here.n * rows, rows)].astype(F32)
        wait_bytes(self.recv, self.rs.at[0])
        for k in range(7):
            mine = mine + self.recv[k].astype(F32)
        return mine

    def gather(self, mine):
        rows, here = self.rows, self.here
        at = ds(here.n * rows, rows)
        self.full[at] = mine.astype(BF)
        for k in (4, 3, 5, 2, 6, 1, 7):
            send(self.full.at[at], self.full.at[at], self.ss.at[1], self.rs.at[1], here.y_peer(k))
        wait_bytes(self.recv, self.rs.at[1])
        self.gathers = True
        return self.full

    def drain(self):
        wait_bytes(self.recv, self.ss.at[0])
        if self.gathers:
            wait_bytes(self.recv, self.ss.at[1])


NB = 32


def inverse_factor(x_ref):
    row = lax.broadcasted_iota(jnp.int32, (NB, 2 * NB), 0)
    col = lax.broadcasted_iota(jnp.int32, (NB, 2 * NB), 1)
    eye = (col == row + NB).astype(F32)
    for b in range(R // NB):
        lo, hi = b * NB, (b + 1) * NB
        block = x_ref[lo:hi, lo:hi]
        e = jnp.concatenate([block, jnp.zeros((NB, NB), F32)], axis=1) + eye
        for j in range(NB - 1):
            pivot = e[j:j + 1, :]
            ratio = e[:, j:j + 1] * (1.0 / e[j:j + 1, j:j + 1])
            e = e - jnp.where(row > j, ratio, 0.0) * pivot
        diag = jnp.sum(jnp.where(row == col, e, 0.0), axis=1, keepdims=True)
        m = e[:, NB:] * lax.rsqrt(diag)
        rows = dot_exact(m, x_ref[lo:hi, :])
        lanes = lax.broadcasted_iota(jnp.int32, (NB, R), 1)
        here = (lanes >= lo) & (lanes < hi)
        wide_m = jnp.concatenate(
            ([jnp.zeros((NB, lo), F32)] if lo else []) + [m] + ([jnp.zeros((NB, R - hi), F32)] if hi < R else []),
            axis=1,
        )
        out = jnp.where(here, wide_m, rows)
        x_ref[lo:hi, :] = out
        if hi < R:
            lower = rows.T[hi:, :]
            rest = x_ref[hi:, :]
            lane = lax.broadcasted_iota(jnp.int32, (R - hi, R), 1)
            rest = jnp.where((lane >= lo) & (lane < hi), 0.0, rest)
            x_ref[hi:, :] = rest - dot_exact(lower, out)


def kernel(w_ref, u_ref, s_ref, basis_ref, proj_ref, *scratch):
    here = Place()
    scratch = list(scratch)
    sums, nsums = [], []
    for lay in WIDE:
        sums.append(WideSum(lay, here, scratch[:11]))
        scratch = scratch[11:]
    for spec in NARROW:
        nsums.append(NarrowSum(spec, here, scratch[:6]))
        scratch = scratch[6:]
    t_ref, y_ref, x_ref = scratch

    barrier = pltpu.get_barrier_semaphore()
    peers = [here.sibling]
    peers += [here.x_peer(k) for k in range(1, NX)]
    peers += [here.z_peer(k) for k in range(1, NZ)]
    peers += [here.y_peer(k) for k in range(1, NY)]
    for peer in peers:
        pl.semaphore_signal(barrier, inc=1, device_id=peer, device_id_type=MESH)

    def enter():
        pl.semaphore_wait(barrier, len(peers))

    def rows_of(ref, size):
        return lambda c: ref[ds(c * size, size), :]

    w_half = rows_of(w_ref, 512)
    t_half = rows_of(t_ref, 128)

    s1 = sums[0]
    s1.start(lambda c: dot(w_half(c), s_ref[...]), enter)
    image = s1.gather()
    n1 = nsums[0]
    mine = n1.scatter(dot(u_ref[...], image[...]))
    whitened = n1.gather(mine)
    t_ref[...] = whitened[...].astype(F32).T.astype(BF)
    s2 = sums[1]
    s2.start(lambda c: dot(t_half(c), u_ref[...]))
    back = s2.gather()
    n2 = nsums[1]
    mine = n2.scatter(dot(back[...], w_ref[...]))
    feature = n2.gather(mine)
    s3 = sums[2]

    def second(c):
        return lax.dot_general(
            w_half(c), feature[...], (((1,), (1,)), ((), ())), preferred_element_type=F32
        )

    s3.start(second)
    image = s3.gather()
    n3 = nsums[2]
    mine = n3.scatter(dot(u_ref[...], image[...]))
    y_ref[...] = mine.astype(BF).astype(F32)
    final = n3.gather(mine)
    t_ref[...] = final[...].astype(F32).T.astype(BF)
    s4, s5 = sums[3], sums[4]
    s4.start(lambda c: dot(t_half(c), final[...]))
    s5.start(lambda c: dot(t_half(c), u_ref[...]))
    for step in ("x_step", "z_step", "z_back", "x_back", "core_back", "finish"):
        getattr(s4, step)()
        getattr(s5, step)()
    x_ref[...] = s4.full[...]
    inverse_factor(x_ref)
    rr = lax.broadcasted_iota(jnp.int32, (R, R), 0)
    cc = lax.broadcasted_iota(jnp.int32, (R, R), 1)
    inverse = jnp.where(cc <= rr, x_ref[...], 0.0)
    x_ref[...] = inverse
    basis_ref[...] = dot_exact(y_ref[...], inverse.T) * math.sqrt(D)
    high = inverse.astype(BF)
    low = (inverse - high.astype(F32)).astype(BF)
    raw = s5.full[...]
    weighted = (dot(high, raw) + dot(low, raw)).astype(BF)
    n4 = nsums[3]
    proj_ref[...] = n4.scatter(dot(weighted, w_ref[...]))
    for s in sums + nsums:
        s.drain()


def on_device(weight, whitening, sketch):
    vmem = pl.BlockSpec(memory_space=pltpu.VMEM)
    scratch = []
    for lay in WIDE:
        scratch += wide_scratch(lay)
    for spec in NARROW:
        scratch += narrow_scratch(spec)
    scratch += [pltpu.VMEM((256, 128), BF), pltpu.VMEM((16, 256), F32), pltpu.VMEM((R, R), F32)]
    return pl.pallas_call(
        kernel,
        out_shape=(
            jax.ShapeDtypeStruct((16, 256), F32),
            jax.ShapeDtypeStruct((32, 832), F32),
        ),
        in_specs=[vmem] * 3,
        out_specs=(vmem, vmem),
        scratch_shapes=scratch,
        compiler_params=pltpu.CompilerParams(
            collective_id=0, has_side_effects=True, vmem_limit_bytes=48 * 1024 * 1024
        ),
        cost_estimate=pl.CostEstimate(flops=2_300_000_000, bytes_accessed=3_000_000, transcendentals=256),
    )(weight, whitening, sketch)


def solution(mesh):
    placed = (P("narrow", "wide"), P("wide", "narrow"), P("wide", None))
    return jax.shard_map(
        on_device,
        mesh=mesh,
        in_specs=placed,
        out_specs=(P(("wide", "narrow"), None), P("narrow", "wide")),
        check_vma=False,
    )
```

```python
import math

import jax
import jax.numpy as jnp
from jax import lax
from jax.experimental import pallas as pl
from jax.experimental.pallas import tpu as pltpu
from jax.sharding import PartitionSpec as P

D = 8192
R = 256
H = 128
NX, NZ, NY = 4, 8, 8
CHAINS = 2
M = H // CHAINS
BF = jnp.bfloat16
F32 = jnp.float32
MESH = pl.DeviceIdType.MESH
FAR_FIRST = (4, 3, 5, 2, 6, 1, 7)
ROUNDS = ("x_step", "z_step", "z_back", "x_back", "finish")


def ds(start, size):
    if isinstance(start, int):
        return pl.ds(start, size)
    return pl.ds(pl.multiple_of(start, size), size)


def dot(a, b):
    return jnp.dot(a, b, preferred_element_type=F32)


def dot_nt(a, b):
    return lax.dot_general(a, b, (((1,), (1,)), ((), ())), preferred_element_type=F32)


def dot_tn(a, b):
    return lax.dot_general(a, b, (((0,), (0,)), ((), ())), preferred_element_type=F32)


def dot_exact(a, b):
    return jnp.dot(a, b, preferred_element_type=F32, precision=lax.Precision.HIGHEST)


class Place:
    def __init__(self):
        w = lax.axis_index("wide")
        self.n = lax.axis_index("narrow")
        self.core = w % 2
        self.x = (w // 2) % NX
        self.z = w // (2 * NX)

    def wide(self, z, x, core):
        return {"wide": (z * NX + x) * 2 + core}

    @property
    def sibling(self):
        return self.wide(self.z, self.x, 1 - self.core)

    def x_peer(self, k):
        return self.wide(self.z, (self.x + k) % NX, self.core)

    def z_peer(self, k):
        return self.wide((self.z + k) % NZ, self.x, self.core)

    def y_peer(self, k):
        return {"narrow": (self.n + k) % NY}


def send(src, dst, ssem, rsem, where):
    copy = pltpu.make_async_remote_copy(
        src_ref=src, dst_ref=dst, send_sem=ssem, recv_sem=rsem, device_id=where, device_id_type=MESH
    )
    copy.start()


def wait_bytes(ref, sem):
    pltpu.make_async_copy(ref, ref, sem).wait()


class Cols:
    dtype = BF

    def __init__(self, base, m):
        self.base, self.m, self.rows = base, m, m // NX
        self.xc, self.zc = (m // NX, 1024), (m // NX, 128)

    def x_of(self, q):
        return (ds(self.base + q * self.rows, self.rows), slice(None))

    def z_of(self, q):
        return (slice(None), ds(q * 128, 128))

    def f_z(self, x, z):
        return (ds(self.base + x * self.rows, self.rows), ds(z * 128, 128))


class Gram:
    dtype, xc, zc = F32, (32, 256), (8, 128)

    def x_of(self, q):
        return (ds(q * 32, 32), slice(None))

    def z_of(self, q):
        return (ds((q // 2) * 8, 8), ds((q % 2) * 128, 128))

    def f_z(self, x, z):
        return (ds(x * 32 + (z // 2) * 8, 8), ds((z % 2) * 128, 128))


def wide_scratch(lay):
    vm = pltpu.VMEM
    return [
        vm((3,) + lay.xc, lay.dtype),
        vm((3,) + lay.xc, lay.dtype),
        vm(lay.xc, F32),
        vm(lay.xc, lay.dtype),
        vm((7,) + lay.zc, lay.dtype),
        pltpu.SemaphoreType.DMA((4,)),
        pltpu.SemaphoreType.DMA((4,)),
    ]


class WideSum:
    def __init__(self, lay, here, bufs, part, full, extra=None):
        self.lay, self.here, self.part, self.full, self.extra = lay, here, part, full, extra
        self.xsend, self.xrecv, self.own, self.zsend, self.zrecv, self.ss, self.rs = bufs
        self.done = 0

    def x_step(self):
        lay, here = self.lay, self.here
        for k in (2, 1, 3, 0):
            q = lay.x_of((here.x + k) % NX)
            total = self.part[q]
            if self.extra is not None:
                total = total + self.extra[q].astype(F32)
            if k:
                self.xsend[k - 1] = total.astype(lay.dtype)
                send(self.xsend.at[k - 1], self.xrecv.at[k - 1], self.ss.at[0], self.rs.at[0], here.x_peer(k))
            else:
                self.own[...] = total
        self.done = 1

    def z_step(self):
        lay, here = self.lay, self.here
        wait_bytes(self.xrecv, self.rs.at[0])
        total = self.own[...]
        for k in range(3):
            total = total + self.xrecv[k].astype(F32)
        self.own[...] = total
        self.zsend[...] = total.astype(lay.dtype)
        for k in FAR_FIRST:
            send(self.zsend.at[lay.z_of((here.z + k) % NZ)], self.zrecv.at[k - 1],
                 self.ss.at[1], self.rs.at[1], here.z_peer(k))
        self.done = 2

    def z_back(self):
        lay, here = self.lay, self.here
        wait_bytes(self.zrecv, self.rs.at[1])
        total = self.own[lay.z_of(here.z)]
        for k in range(7):
            total = total + self.zrecv[k].astype(F32)
        mine = lay.f_z(here.x, here.z)
        self.full[mine] = total.astype(lay.dtype)
        for k in FAR_FIRST:
            send(self.full.at[mine], self.full.at[mine], self.ss.at[2], self.rs.at[2], here.z_peer(k))
        self.done = 3

    def x_back(self):
        lay, here = self.lay, self.here
        wait_bytes(self.zrecv, self.rs.at[2])
        mine = lay.x_of(here.x)
        for k in (2, 1, 3):
            send(self.full.at[mine], self.full.at[mine], self.ss.at[3], self.rs.at[3], here.x_peer(k))
        self.done = 4

    def finish(self):
        wait_bytes(self.xrecv, self.rs.at[3])
        self.done = 5

    def drain(self):
        for i, ref in enumerate((self.xrecv, self.zrecv, self.zrecv, self.xrecv)):
            if self.done > i:
                wait_bytes(ref, self.ss.at[i])
                if self.done == i + 1:
                    wait_bytes(ref, self.rs.at[i])


def narrow_scratch(width):
    return [
        pltpu.VMEM((H, width), BF),
        pltpu.VMEM((7, 16, width), BF),
        pltpu.SemaphoreType.DMA((2,)),
        pltpu.SemaphoreType.DMA((2,)),
    ]


class NarrowSum:
    def __init__(self, here, bufs, full, base=0):
        self.here, self.full, self.base = here, full, base
        self.sendbuf, self.recv, self.ss, self.rs = bufs
        self.done = 0

    def scatter(self, total):
        here = self.here
        self.sendbuf[...] = total.astype(BF)
        for k in FAR_FIRST:
            send(self.sendbuf.at[ds(((here.n + k) % NY) * 16, 16)], self.recv.at[k - 1],
                 self.ss.at[0], self.rs.at[0], here.y_peer(k))
        self.done = 1

    def gather(self):
        here = self.here
        mine = self.sendbuf[ds(here.n * 16, 16)].astype(F32)
        wait_bytes(self.recv, self.rs.at[0])
        for k in range(7):
            mine = mine + self.recv[k].astype(F32)
        at = ds(self.base + here.n * 16, 16)
        self.full[at] = mine.astype(BF)
        for k in FAR_FIRST:
            send(self.full.at[at], self.full.at[at], self.ss.at[1], self.rs.at[1], here.y_peer(k))
        self.done = 2

    def finish(self):
        wait_bytes(self.recv, self.rs.at[1])
        self.done = 3

    def drain(self):
        for i in range(2):
            if self.done > i:
                wait_bytes(self.recv, self.ss.at[i])
                if self.done == i + 1:
                    wait_bytes(self.recv, self.rs.at[i])


NB = 32


def inverse_factor(x_ref):
    row = lax.broadcasted_iota(jnp.int32, (NB, 2 * NB), 0)
    col = lax.broadcasted_iota(jnp.int32, (NB, 2 * NB), 1)
    eye = (col == row + NB).astype(F32)
    for b in range(R // NB):
        lo, hi = b * NB, (b + 1) * NB
        block = x_ref[lo:hi, lo:hi]
        e = jnp.concatenate([block, jnp.zeros((NB, NB), F32)], axis=1) + eye
        for j in range(NB - 1):
            pivot = e[j:j + 1, :]
            ratio = e[:, j:j + 1] * (1.0 / e[j:j + 1, j:j + 1])
            e = e - jnp.where(row > j, ratio, 0.0) * pivot
        diag = jnp.sum(jnp.where(row == col, e, 0.0), axis=1, keepdims=True)
        m = e[:, NB:] * lax.rsqrt(diag)
        rows = dot_exact(m, x_ref[lo:hi, :])
        lanes = lax.broadcasted_iota(jnp.int32, (NB, R), 1)
        wide_m = jnp.concatenate(
            ([jnp.zeros((NB, lo), F32)] if lo else []) + [m] + ([jnp.zeros((NB, R - hi), F32)] if hi < R else []),
            axis=1,
        )
        out = jnp.where((lanes >= lo) & (lanes < hi), wide_m, rows)
        x_ref[lo:hi, :] = out
        if hi < R:
            lower = rows.T[hi:, :]
            rest = x_ref[hi:, :]
            lane = lax.broadcasted_iota(jnp.int32, (R - hi, R), 1)
            rest = jnp.where((lane >= lo) & (lane < hi), 0.0, rest)
            x_ref[hi:, :] = rest - dot_exact(lower, out)
        yield b


CHAIN = [Cols(g * M, M) for g in range(CHAINS)]
ONE = Cols(0, H)
WIDE = CHAIN + CHAIN + CHAIN + [ONE, Gram()]
NARROW = (256, 832, 832, 256)


def body(wt_hbm, u_hbm, s_hbm, basis_ref, proj_ref, scratch, drains):
    here = Place()
    core, n = here.core, here.n
    scratch = list(scratch)

    def take(count):
        got = scratch[:count]
        del scratch[:count]
        return got

    wide_bufs = [take(7) for _ in WIDE]
    narrow_bufs = [take(4) for _ in NARROW]
    (wt2, u2, s_ref, csend, crecv, part, img1, img2, img3, img4, gpart, gfull, v_ref, c2, ya, yb, x_ref,
     zbuf, zrecv, zpair, zall, pbuf, precv) = take(23)
    lsem, psem, qsem = take(3)

    barrier = pltpu.get_barrier_semaphore()
    peers = [here.sibling]
    peers += [here.x_peer(k) for k in range(1, NX)]
    peers += [here.z_peer(k) for k in range(1, NZ)]
    peers += [here.y_peer(k) for k in range(1, NY)]
    for peer in peers:
        pl.semaphore_signal(barrier, inc=1, device_id=peer, device_id_type=MESH)
    loads = [
        pltpu.make_async_copy(wt_hbm, wt2.at[core], lsem.at[0]),
        pltpu.make_async_copy(s_hbm, s_ref, lsem.at[1]),
        pltpu.make_async_copy(u_hbm, u2.at[ds(core * H, H)], lsem.at[2]),
    ]
    for load in loads:
        load.start()
    zbuf[...] = jnp.zeros_like(zbuf)
    for load in loads:
        load.wait()

    def first(c):
        return dot_tn(s_ref[:, ds(c * H, H)], wt2[core])

    csend[...] = first(1 - core).astype(BF)
    pl.semaphore_wait(barrier, len(peers))
    send(csend, crecv, psem.at[0], qsem.at[0], here.sibling)
    mine_u = u2.at[ds(core * H, H)]
    send(wt2.at[core], wt2.at[core], psem.at[1], qsem.at[1], here.sibling)
    send(mine_u, mine_u, psem.at[2], qsem.at[2], here.sibling)
    drains.append(lambda: wait_bytes(csend, psem.at[0]))
    drains.append(lambda: wait_bytes(wt2.at[0], psem.at[1]))
    drains.append(lambda: wait_bytes(u2.at[0:H], psem.at[2]))
    part[...] = first(core)
    wait_bytes(crecv, qsem.at[0])
    yield "start"

    sums = []

    def wide(index, full, parts=part, extra=None):
        got = WideSum(WIDE[index], here, wide_bufs[index], parts, full, extra)
        drains.append(got.drain)
        return got

    def run(chain):
        for step in ROUNDS:
            for s in chain:
                getattr(s, step)()
            yield step

    def narrow(index, full, base=0):
        got = NarrowSum(here, narrow_bufs[index], full, base)
        drains.append(got.drain)
        return got

    yield from run([wide(g, img1, extra=crecv) for g in range(CHAINS)])
    wait_bytes(u2.at[0:H], qsem.at[2])
    n1 = narrow(0, v_ref)
    n1.scatter(dot_nt(img1[...], u2[...]))
    yield "n1s"
    n1.gather()
    yield "n1g"
    n1.finish()
    part[...] = dot(v_ref[...], u2[...])
    yield from run([wide(CHAINS + g, img2) for g in range(CHAINS)])
    wait_bytes(wt2.at[0], qsem.at[1])
    n2 = [narrow(1 + b, c2.at[b]) for b in range(2)]
    for b in range(2):
        n2[b].scatter(dot_nt(img2[...], wt2[b]))
    yield "n2s"
    for b in range(2):
        n2[b].gather()
    yield "n2g"
    n2[0].finish()
    part[...] = dot(c2[0], wt2[0])
    n2[1].finish()
    part[...] += dot(c2[1], wt2[1])
    yield from run([wide(2 * CHAINS + g, img3) for g in range(CHAINS)])
    n3 = narrow(3, ya, core * H)
    n3.scatter(dot_nt(img3[...], u2[...]))
    yield "n3s"
    n3.gather()
    yield "n3g"
    n3.finish()
    mine_y = ya.at[ds(core * H, H)]
    send(mine_y, mine_y, psem.at[3], qsem.at[3], here.sibling)
    drains.append(lambda: wait_bytes(ya.at[0:H], psem.at[3]))
    part[...] = dot(mine_y[...], u2[...])
    wait_bytes(ya.at[0:H], qsem.at[3])
    gpart[...] = dot_nt(mine_y[...], ya[...])
    gfull_mine = gfull.at[ds(core * H, H)]
    gram = wide(3 * CHAINS + 1, gfull_mine, gpart)
    last = wide(3 * CHAINS, img4)
    yield "y"
    gram.x_step()
    last.x_step()
    yb[...] = ya[...].astype(F32).T
    yield "gx"
    gram.z_step()
    last.z_step()
    yield "gz"
    gram.z_back()
    last.z_back()
    yield "gzb"
    gram.x_back()
    last.x_back()
    yield "gxb"
    gram.finish()
    send(gfull_mine, gfull_mine, psem.at[4], qsem.at[4], here.sibling)
    drains.append(lambda: wait_bytes(gfull.at[0:H], psem.at[4]))
    wait_bytes(gfull.at[0:H], qsem.at[4])
    yield "gram"
    x_ref[...] = gfull[...]
    factor = inverse_factor(x_ref)
    next(factor)
    last.finish()
    for b in range(2):
        zbuf[b, :, 0:832] = dot_nt(img4[...], wt2[b]).astype(BF)
    for k in FAR_FIRST:
        to = (n + k) % NY

        @pl.when(to < 7)
        def _():
            send(zbuf.at[:, :, ds(to * 128, 128)], zrecv.at[k - 1], psem.at[5], qsem.at[5], here.y_peer(k))

    def drain_z():
        @pl.when(n < 7)
        def _():
            wait_bytes(zrecv.at[0:6], psem.at[5])

        @pl.when(n == 7)
        def _():
            wait_bytes(zrecv, psem.at[5])

    drains.append(drain_z)
    for _ in range(5):
        next(factor)

    @pl.when(n < 7)
    def _():
        wait_bytes(zrecv, qsem.at[5])
        total = zbuf[:, :, ds(n * 128, 128)].astype(F32)
        for k in range(7):
            total = total + zrecv[k].astype(F32)
        zpair[...] = total.astype(BF)
        to = zall.at[ds(core * H, H)]
        send(zpair.at[1 - core], to, psem.at[6], qsem.at[6], here.sibling)
        to[...] = zpair[core]

    for _ in factor:
        pass
    rr = lax.broadcasted_iota(jnp.int32, (R, R), 0)
    cc = lax.broadcasted_iota(jnp.int32, (R, R), 1)
    inverse = jnp.where(cc <= rr, x_ref[...], 0.0)
    yield "factor"
    high = inverse.astype(BF)
    low = (inverse - high.astype(F32)).astype(BF)

    @pl.when(n < 7)
    def _():
        wait_bytes(zpair.at[0], qsem.at[6])
        pbuf[...] = (dot(high, zall[...]) + dot(low, zall[...])).astype(BF)
        for k in FAR_FIRST:
            send(pbuf.at[ds(((n + k) % NY) * 32, 32)], precv.at[n], psem.at[7], qsem.at[7], here.y_peer(k))
        precv[n] = pbuf[ds(n * 32, 32)]

    rows = yb[ds(core * H + n * 16, 16), :]
    basis_ref[...] = lax.dot_general(
        rows, inverse, (((1,), (1,)), ((), ())), preferred_element_type=F32, precision=lax.Precision.HIGHEST
    ) * math.sqrt(D)

    @pl.when(n < 7)
    def _():
        wait_bytes(precv.at[0:6], qsem.at[7])

    @pl.when(n == 7)
    def _():
        wait_bytes(precv, qsem.at[7])

    for j in range(6):
        proj_ref[:, j * 128:(j + 1) * 128] = precv[j].astype(F32)
    proj_ref[:, 768:832] = precv[6][:, 0:64].astype(F32)

    @pl.when(n < 7)
    def _():
        wait_bytes(zpair.at[0], psem.at[6])
        wait_bytes(precv, psem.at[7])

    yield "end"


def kernel(wt_hbm, u_hbm, s_hbm, basis_ref, proj_ref, *scratch):
    drains = []
    for _ in body(wt_hbm, u_hbm, s_hbm, basis_ref, proj_ref, scratch, drains):
        pass
    for drain in drains:
        drain()


def on_device(weight, whitening, sketch):
    vmem = pl.BlockSpec(memory_space=pltpu.VMEM)
    hbm = pl.BlockSpec(memory_space=pl.ANY)
    vm = pltpu.VMEM
    scratch = []
    for lay in WIDE:
        scratch += wide_scratch(lay)
    for width in NARROW:
        scratch += narrow_scratch(width)
    scratch += [
        vm((2, 832, 1024), BF),
        vm((2 * H, 1024), BF),
        vm((832, R), BF),
        vm((H, 1024), BF),
        vm((H, 1024), BF),
        vm((H, 1024), F32),
        vm((H, 1024), BF),
        vm((H, 1024), BF),
        vm((H, 1024), BF),
        vm((H, 1024), BF),
        vm((H, R), F32),
        vm((R, R), F32),
        vm((H, 2 * H), BF),
        vm((2, H, 832), BF),
        vm((R, 2 * H), BF),
        vm((2 * H, R), F32),
        vm((R, R), F32),
        vm((2, H, 896), BF),
        vm((7, 2, H, 128), BF),
        vm((2, H, 128), BF),
        vm((R, 128), BF),
        vm((R, 128), BF),
        vm((7, 32, 128), BF),
        pltpu.SemaphoreType.DMA((3,)),
        pltpu.SemaphoreType.DMA((8,)),
        pltpu.SemaphoreType.DMA((8,)),
    ]
    return pl.pallas_call(
        kernel,
        out_shape=(
            jax.ShapeDtypeStruct((16, R), F32),
            jax.ShapeDtypeStruct((32, 832), F32),
        ),
        in_specs=[hbm] * 3,
        out_specs=(vmem, vmem),
        scratch_shapes=scratch,
        compiler_params=pltpu.CompilerParams(
            collective_id=0, has_side_effects=True, vmem_limit_bytes=48 * 1024 * 1024
        ),
        cost_estimate=pl.CostEstimate(flops=2_300_000_000, bytes_accessed=3_000_000, transcendentals=256),
    )(weight.T, whitening, sketch)


def solution(mesh):
    placed = (P("narrow", "wide"), P("wide", "narrow"), P("wide", None))
    return jax.shard_map(
        on_device,
        mesh=mesh,
        in_specs=placed,
        out_specs=(P(("wide", "narrow"), None), P("narrow", "wide")),
        check_vma=False,
    )
```

```python
import math

import jax
import jax.numpy as jnp
from jax import lax
from jax.experimental import pallas as pl
from jax.experimental.pallas import tpu as pltpu
from jax.sharding import PartitionSpec as P

D = 8192
R = 256
H = 128
NX, NZ, NY = 4, 8, 8
CHAINS = 2
M = H // CHAINS
BF = jnp.bfloat16
F32 = jnp.float32
MESH = pl.DeviceIdType.MESH
FAR_FIRST = (4, 3, 5, 2, 6, 1, 7)
ROUNDS = ("x_step", "z_step", "z_back", "x_back", "finish")


def ds(start, size):
    if isinstance(start, int):
        return pl.ds(start, size)
    return pl.ds(pl.multiple_of(start, size), size)


def dot(a, b):
    return jnp.dot(a, b, preferred_element_type=F32)


def dot_nt(a, b):
    return lax.dot_general(a, b, (((1,), (1,)), ((), ())), preferred_element_type=F32)


def dot_tn(a, b):
    return lax.dot_general(a, b, (((0,), (0,)), ((), ())), preferred_element_type=F32)


class Place:
    def __init__(self):
        w = lax.axis_index("wide")
        self.n = lax.axis_index("narrow")
        self.core = w % 2
        self.x = (w // 2) % NX
        self.z = w // (2 * NX)

    def wide(self, z, x, core):
        return {"wide": (z * NX + x) * 2 + core}

    @property
    def sibling(self):
        return self.wide(self.z, self.x, 1 - self.core)

    def x_peer(self, k):
        return self.wide(self.z, (self.x + k) % NX, self.core)

    def z_peer(self, k):
        return self.wide((self.z + k) % NZ, self.x, self.core)

    def y_peer(self, k):
        return {"narrow": (self.n + k) % NY}


def send(src, dst, ssem, rsem, where):
    copy = pltpu.make_async_remote_copy(
        src_ref=src, dst_ref=dst, send_sem=ssem, recv_sem=rsem, device_id=where, device_id_type=MESH
    )
    copy.start()


def wait_bytes(ref, sem):
    pltpu.make_async_copy(ref, ref, sem).wait()


class Cols:
    dtype = BF

    def __init__(self, base, m):
        self.base, self.m, self.rows = base, m, m // NX
        self.xc, self.zc = (m // NX, 1024), (m // NX, 128)

    def x_of(self, q):
        return (ds(self.base + q * self.rows, self.rows), slice(None))

    def z_of(self, q):
        return (slice(None), ds(q * 128, 128))

    def f_z(self, x, z):
        return (ds(self.base + x * self.rows, self.rows), ds(z * 128, 128))


class Gram:
    dtype, xc, zc = F32, (32, 256), (8, 128)

    def x_of(self, q):
        return (ds(q * 32, 32), slice(None))

    def z_of(self, q):
        return (ds((q // 2) * 8, 8), ds((q % 2) * 128, 128))

    def f_z(self, x, z):
        return (ds(x * 32 + (z // 2) * 8, 8), ds((z % 2) * 128, 128))


def wide_scratch(lay):
    vm = pltpu.VMEM
    return [
        vm((3,) + lay.xc, lay.dtype),
        vm((3,) + lay.xc, lay.dtype),
        vm(lay.xc, F32),
        vm(lay.xc, lay.dtype),
        vm((7,) + lay.zc, lay.dtype),
        pltpu.SemaphoreType.DMA((4,)),
        pltpu.SemaphoreType.DMA((4,)),
    ]


class WideSum:
    def __init__(self, lay, here, bufs, part, full, extra=None):
        self.lay, self.here, self.part, self.full, self.extra = lay, here, part, full, extra
        self.xsend, self.xrecv, self.own, self.zsend, self.zrecv, self.ss, self.rs = bufs
        self.done = 0

    def x_step(self):
        lay, here = self.lay, self.here
        for k in (2, 1, 3, 0):
            q = lay.x_of((here.x + k) % NX)
            total = self.part[q]
            if self.extra is not None:
                total = total + self.extra[q].astype(F32)
            if k:
                self.xsend[k - 1] = total.astype(lay.dtype)
                send(self.xsend.at[k - 1], self.xrecv.at[k - 1], self.ss.at[0], self.rs.at[0], here.x_peer(k))
            else:
                self.own[...] = total
        self.done = 1

    def z_step(self):
        lay, here = self.lay, self.here
        wait_bytes(self.xrecv, self.rs.at[0])
        total = self.own[...]
        for k in range(3):
            total = total + self.xrecv[k].astype(F32)
        self.own[...] = total
        self.zsend[...] = total.astype(lay.dtype)
        for k in FAR_FIRST:
            send(self.zsend.at[lay.z_of((here.z + k) % NZ)], self.zrecv.at[k - 1],
                 self.ss.at[1], self.rs.at[1], here.z_peer(k))
        self.done = 2

    def z_back(self):
        lay, here = self.lay, self.here
        wait_bytes(self.zrecv, self.rs.at[1])
        total = self.own[lay.z_of(here.z)]
        for k in range(7):
            total = total + self.zrecv[k].astype(F32)
        mine = lay.f_z(here.x, here.z)
        self.full[mine] = total.astype(lay.dtype)
        for k in FAR_FIRST:
            send(self.full.at[mine], self.full.at[mine], self.ss.at[2], self.rs.at[2], here.z_peer(k))
        self.done = 3

    def x_back(self):
        lay, here = self.lay, self.here
        wait_bytes(self.zrecv, self.rs.at[2])
        mine = lay.x_of(here.x)
        for k in (2, 1, 3):
            send(self.full.at[mine], self.full.at[mine], self.ss.at[3], self.rs.at[3], here.x_peer(k))
        self.done = 4

    def finish(self):
        wait_bytes(self.xrecv, self.rs.at[3])
        self.done = 5

    def drain(self):
        for i, ref in enumerate((self.xrecv, self.zrecv, self.zrecv, self.xrecv)):
            if self.done > i:
                wait_bytes(ref, self.ss.at[i])
                if self.done == i + 1:
                    wait_bytes(ref, self.rs.at[i])


def narrow_scratch(width):
    return [
        pltpu.VMEM((H, width), BF),
        pltpu.VMEM((7, 16, width), BF),
        pltpu.SemaphoreType.DMA((2,)),
        pltpu.SemaphoreType.DMA((2,)),
    ]


class NarrowSum:
    def __init__(self, here, bufs, full, base=0):
        self.here, self.full, self.base = here, full, base
        self.sendbuf, self.recv, self.ss, self.rs = bufs
        self.done = 0

    def scatter(self, total):
        here = self.here
        self.sendbuf[...] = total.astype(BF)
        for k in FAR_FIRST:
            send(self.sendbuf.at[ds(((here.n + k) % NY) * 16, 16)], self.recv.at[k - 1],
                 self.ss.at[0], self.rs.at[0], here.y_peer(k))
        self.done = 1

    def gather(self):
        here = self.here
        mine = self.sendbuf[ds(here.n * 16, 16)].astype(F32)
        wait_bytes(self.recv, self.rs.at[0])
        for k in range(7):
            mine = mine + self.recv[k].astype(F32)
        at = ds(self.base + here.n * 16, 16)
        self.full[at] = mine.astype(BF)
        for k in FAR_FIRST:
            send(self.full.at[at], self.full.at[at], self.ss.at[1], self.rs.at[1], here.y_peer(k))
        self.done = 2

    def finish(self):
        wait_bytes(self.recv, self.rs.at[1])
        self.done = 3

    def drain(self):
        for i in range(2):
            if self.done > i:
                wait_bytes(self.recv, self.ss.at[i])
                if self.done == i + 1:
                    wait_bytes(self.recv, self.rs.at[i])


NB = 32
GROUP = 8


def thirds(a):
    first = a.astype(BF)
    rest = a - first.astype(F32)
    second = rest.astype(BF)
    return first, second, (rest - second.astype(F32)).astype(BF)


def dot_thirds(a, b):
    a1, a2, a3 = thirds(a)
    b1, b2, b3 = thirds(b)
    return dot(
        jnp.concatenate([a1, a1, a2, a2, a1, a3], axis=1),
        jnp.concatenate([b1, b2, b1, b2, b3, b1], axis=0),
    )


def block_inverse(block):
    shape = (NB, 2 * NB)
    row = lax.broadcasted_iota(jnp.int32, shape, 0)
    col = lax.broadcasted_iota(jnp.int32, shape, 1)
    e = jnp.concatenate([block, jnp.zeros((NB, NB), F32)], axis=1) + (col == row + NB).astype(F32)
    for start in range(0, NB, GROUP):
        spread = [jnp.broadcast_to(e[:, start + j:start + j + 1], shape) for j in range(GROUP)]
        for p in range(GROUP):
            at = slice(start + p, start + p + 1)
            ratio = jnp.where(row > start + p, spread[p] * (1.0 / spread[p][at]), 0.0)
            for m in range(p + 1, GROUP):
                spread[m] = spread[m] - ratio * spread[m][at]
            e = e - ratio * e[at]
    diagonal = jnp.sum(jnp.where(row == col, e, 0.0), axis=1, keepdims=True)
    return e[:, NB:] * lax.rsqrt(diagonal)


def inverse_factor(x_ref):
    for b in range(R // NB):
        lo, hi = b * NB, (b + 1) * NB
        m = block_inverse(x_ref[lo:hi, lo:hi])
        rows = dot_thirds(m, x_ref[lo:hi, :])
        lane = lax.broadcasted_iota(jnp.int32, (NB, R), 1)
        pieces = [jnp.zeros((NB, lo), F32)] if lo else []
        pieces.append(m)
        if hi < R:
            pieces.append(jnp.zeros((NB, R - hi), F32))
        out = jnp.where((lane >= lo) & (lane < hi), jnp.concatenate(pieces, axis=1), rows)
        x_ref[lo:hi, :] = out
        if hi < R:
            lane = lax.broadcasted_iota(jnp.int32, (R - hi, R), 1)
            rest = jnp.where((lane >= lo) & (lane < hi), 0.0, x_ref[hi:, :])
            x_ref[hi:, :] = rest - dot_thirds(rows.T[hi:, :], out)
        yield b


CHAIN = [Cols(g * M, M) for g in range(CHAINS)]
ONE = Cols(0, H)
WIDE = CHAIN + CHAIN + CHAIN + [ONE, Gram()]
NARROW = (256, 832, 832, 256)


def body(wt_hbm, u_hbm, s_hbm, basis_ref, proj_ref, scratch, drains):
    here = Place()
    core, n = here.core, here.n
    scratch = list(scratch)

    def take(count):
        got = scratch[:count]
        del scratch[:count]
        return got

    wide_bufs = [take(7) for _ in WIDE]
    narrow_bufs = [take(4) for _ in NARROW]
    (wt2, u2, s_ref, csend, crecv, part, img1, img2, img3, img4, gpart, gfull, v_ref, c2, ya, yb, x_ref,
     zbuf, zrecv, zpair, zall, pbuf, precv) = take(23)
    lsem, psem, qsem = take(3)

    barrier = pltpu.get_barrier_semaphore()
    peers = [here.sibling]
    peers += [here.x_peer(k) for k in range(1, NX)]
    peers += [here.z_peer(k) for k in range(1, NZ)]
    peers += [here.y_peer(k) for k in range(1, NY)]
    for peer in peers:
        pl.semaphore_signal(barrier, inc=1, device_id=peer, device_id_type=MESH)
    loads = [
        pltpu.make_async_copy(wt_hbm, wt2.at[core], lsem.at[0]),
        pltpu.make_async_copy(s_hbm, s_ref, lsem.at[1]),
        pltpu.make_async_copy(u_hbm, u2.at[ds(core * H, H)], lsem.at[2]),
    ]
    for load in loads:
        load.start()
    zbuf[...] = jnp.zeros_like(zbuf)
    for load in loads:
        load.wait()

    def first(c):
        return dot_tn(s_ref[:, ds(c * H, H)], wt2[core])

    csend[...] = first(1 - core).astype(BF)
    pl.semaphore_wait(barrier, len(peers))
    send(csend, crecv, psem.at[0], qsem.at[0], here.sibling)
    mine_u = u2.at[ds(core * H, H)]
    send(wt2.at[core], wt2.at[core], psem.at[1], qsem.at[1], here.sibling)
    send(mine_u, mine_u, psem.at[2], qsem.at[2], here.sibling)
    drains.append(lambda: wait_bytes(csend, psem.at[0]))
    drains.append(lambda: wait_bytes(wt2.at[0], psem.at[1]))
    drains.append(lambda: wait_bytes(u2.at[0:H], psem.at[2]))
    part[...] = first(core)
    wait_bytes(crecv, qsem.at[0])
    yield "start"

    sums = []

    def wide(index, full, parts=part, extra=None):
        got = WideSum(WIDE[index], here, wide_bufs[index], parts, full, extra)
        drains.append(got.drain)
        return got

    def run(chain):
        for step in ROUNDS:
            for s in chain:
                getattr(s, step)()
            yield step

    def narrow(index, full, base=0):
        got = NarrowSum(here, narrow_bufs[index], full, base)
        drains.append(got.drain)
        return got

    yield from run([wide(g, img1, extra=crecv) for g in range(CHAINS)])
    wait_bytes(u2.at[0:H], qsem.at[2])
    n1 = narrow(0, v_ref)
    n1.scatter(dot_nt(img1[...], u2[...]))
    yield "n1s"
    n1.gather()
    yield "n1g"
    n1.finish()
    part[...] = dot(v_ref[...], u2[...])
    yield from run([wide(CHAINS + g, img2) for g in range(CHAINS)])
    wait_bytes(wt2.at[0], qsem.at[1])
    n2 = [narrow(1 + b, c2.at[b]) for b in range(2)]
    for b in range(2):
        n2[b].scatter(dot_nt(img2[...], wt2[b]))
    yield "n2s"
    for b in range(2):
        n2[b].gather()
    yield "n2g"
    n2[0].finish()
    part[...] = dot(c2[0], wt2[0])
    n2[1].finish()
    part[...] += dot(c2[1], wt2[1])
    yield from run([wide(2 * CHAINS + g, img3) for g in range(CHAINS)])
    n3 = narrow(3, ya, core * H)
    n3.scatter(dot_nt(img3[...], u2[...]))
    yield "n3s"
    n3.gather()
    yield "n3g"
    n3.finish()
    mine_y = ya.at[ds(core * H, H)]
    send(mine_y, mine_y, psem.at[3], qsem.at[3], here.sibling)
    drains.append(lambda: wait_bytes(ya.at[0:H], psem.at[3]))
    part[...] = dot(mine_y[...], u2[...])
    wait_bytes(ya.at[0:H], qsem.at[3])
    gpart[...] = dot_nt(mine_y[...], ya[...])
    gfull_mine = gfull.at[ds(core * H, H)]
    gram = wide(3 * CHAINS + 1, gfull_mine, gpart)
    last = wide(3 * CHAINS, img4)
    yield "y"
    gram.x_step()
    last.x_step()
    yb[...] = ya[...].astype(F32).T
    yield "gx"
    gram.z_step()
    last.z_step()
    yield "gz"
    gram.z_back()
    last.z_back()
    yield "gzb"
    gram.x_back()
    last.x_back()
    yield "gxb"
    gram.finish()
    send(gfull_mine, gfull_mine, psem.at[4], qsem.at[4], here.sibling)
    drains.append(lambda: wait_bytes(gfull.at[0:H], psem.at[4]))
    wait_bytes(gfull.at[0:H], qsem.at[4])
    yield "gram"
    last.finish()
    for b in range(2):
        zbuf[b, :, 0:832] = dot_nt(img4[...], wt2[b]).astype(BF)
        for k in FAR_FIRST:
            to = (n + k) % NY

            @pl.when(to < 7)
            def _():
                send(zbuf.at[b, :, ds(to * 128, 128)], zrecv.at[b, k - 1], psem.at[5 + b], qsem.at[5 + b], here.y_peer(k))

    def drain_z():
        for b in range(2):

            @pl.when(n < 7)
            def _():
                wait_bytes(zrecv.at[b, 0:6], psem.at[5 + b])

            @pl.when(n == 7)
            def _():
                wait_bytes(zrecv.at[b], psem.at[5 + b])

    drains.append(drain_z)
    x_ref[...] = gfull[...]
    factor = inverse_factor(x_ref)
    for _ in range(5):
        next(factor)

    @pl.when(n < 7)
    def _():
        for b in range(2):
            wait_bytes(zrecv.at[b], qsem.at[5 + b])
            total = zbuf[b, :, ds(n * 128, 128)].astype(F32)
            for k in range(7):
                total = total + zrecv[b, k].astype(F32)
            zpair[b] = total.astype(BF)
        to = zall.at[ds(core * H, H)]
        send(zpair.at[1 - core], to, psem.at[8], qsem.at[8], here.sibling)
        to[...] = zpair[core]

    for _ in factor:
        pass
    rr = lax.broadcasted_iota(jnp.int32, (R, R), 0)
    cc = lax.broadcasted_iota(jnp.int32, (R, R), 1)
    inverse = jnp.where(cc <= rr, x_ref[...], 0.0)
    yield "factor"
    high = inverse.astype(BF)
    low = (inverse - high.astype(F32)).astype(BF)

    @pl.when(n < 7)
    def _():
        wait_bytes(zpair.at[0], qsem.at[8])
        pbuf[...] = (dot(high, zall[...]) + dot(low, zall[...])).astype(BF)
        for k in FAR_FIRST:
            send(pbuf.at[ds(((n + k) % NY) * 32, 32)], precv.at[n], psem.at[7], qsem.at[7], here.y_peer(k))
        precv[n] = pbuf[ds(n * 32, 32)]

    rows = yb[ds(core * H + n * 16, 16), :]
    basis_ref[...] = lax.dot_general(
        rows, inverse, (((1,), (1,)), ((), ())), preferred_element_type=F32, precision=lax.Precision.HIGHEST
    ) * math.sqrt(D)

    @pl.when(n < 7)
    def _():
        wait_bytes(precv.at[0:6], qsem.at[7])

    @pl.when(n == 7)
    def _():
        wait_bytes(precv, qsem.at[7])

    for j in range(6):
        proj_ref[:, j * 128:(j + 1) * 128] = precv[j].astype(F32)
    proj_ref[:, 768:832] = precv[6][:, 0:64].astype(F32)

    @pl.when(n < 7)
    def _():
        wait_bytes(zpair.at[0], psem.at[8])
        wait_bytes(precv, psem.at[7])

    yield "end"


def kernel(wt_hbm, u_hbm, s_hbm, basis_ref, proj_ref, *scratch):
    drains = []
    for _ in body(wt_hbm, u_hbm, s_hbm, basis_ref, proj_ref, scratch, drains):
        pass
    for drain in drains:
        drain()


def on_device(weight, whitening, sketch):
    vmem = pl.BlockSpec(memory_space=pltpu.VMEM)
    hbm = pl.BlockSpec(memory_space=pl.ANY)
    vm = pltpu.VMEM
    scratch = []
    for lay in WIDE:
        scratch += wide_scratch(lay)
    for width in NARROW:
        scratch += narrow_scratch(width)
    scratch += [
        vm((2, 832, 1024), BF),
        vm((2 * H, 1024), BF),
        vm((832, R), BF),
        vm((H, 1024), BF),
        vm((H, 1024), BF),
        vm((H, 1024), F32),
        vm((H, 1024), BF),
        vm((H, 1024), BF),
        vm((H, 1024), BF),
        vm((H, 1024), BF),
        vm((H, R), F32),
        vm((R, R), F32),
        vm((H, 2 * H), BF),
        vm((2, H, 832), BF),
        vm((R, 2 * H), BF),
        vm((2 * H, R), F32),
        vm((R, R), F32),
        vm((2, H, 896), BF),
        vm((2, 7, H, 128), BF),
        vm((2, H, 128), BF),
        vm((R, 128), BF),
        vm((R, 128), BF),
        vm((7, 32, 128), BF),
        pltpu.SemaphoreType.DMA((3,)),
        pltpu.SemaphoreType.DMA((9,)),
        pltpu.SemaphoreType.DMA((9,)),
    ]
    return pl.pallas_call(
        kernel,
        out_shape=(
            jax.ShapeDtypeStruct((16, R), F32),
            jax.ShapeDtypeStruct((32, 832), F32),
        ),
        in_specs=[hbm] * 3,
        out_specs=(vmem, vmem),
        scratch_shapes=scratch,
        compiler_params=pltpu.CompilerParams(
            collective_id=0, has_side_effects=True, vmem_limit_bytes=48 * 1024 * 1024
        ),
        cost_estimate=pl.CostEstimate(flops=2_300_000_000, bytes_accessed=3_000_000, transcendentals=256),
    )(weight.T, whitening, sketch)


def solution(mesh):
    placed = (P("narrow", "wide"), P("wide", "narrow"), P("wide", None))
    return jax.shard_map(
        on_device,
        mesh=mesh,
        in_specs=placed,
        out_specs=(P(("wide", "narrow"), None), P("narrow", "wide")),
        check_vma=False,
    )
```

```python
import math

import jax
import jax.numpy as jnp
from jax import lax
from jax.experimental import pallas as pl
from jax.experimental.pallas import tpu as pltpu
from jax.sharding import PartitionSpec as P

D = 8192
R = 256
H = 128
NX, NZ, NY = 4, 8, 8
CHAINS = 2
M = H // CHAINS
BF = jnp.bfloat16
F32 = jnp.float32
MESH = pl.DeviceIdType.MESH
FAR_FIRST = (4, 3, 5, 2, 6, 1, 7)
ROUNDS = ("x_step", "z_step", "z_back", "x_back", "finish")


def ds(start, size):
    if isinstance(start, int):
        return pl.ds(start, size)
    return pl.ds(pl.multiple_of(start, size), size)


def dot(a, b):
    return jnp.dot(a, b, preferred_element_type=F32)


def dot_nt(a, b):
    return lax.dot_general(a, b, (((1,), (1,)), ((), ())), preferred_element_type=F32)


def dot_tn(a, b):
    return lax.dot_general(a, b, (((0,), (0,)), ((), ())), preferred_element_type=F32)


class Place:
    def __init__(self):
        w = lax.axis_index("wide")
        self.n = lax.axis_index("narrow")
        self.core = w % 2
        self.x = (w // 2) % NX
        self.z = w // (2 * NX)

    def wide(self, z, x, core):
        return {"wide": (z * NX + x) * 2 + core}

    @property
    def sibling(self):
        return self.wide(self.z, self.x, 1 - self.core)

    def x_peer(self, k):
        return self.wide(self.z, (self.x + k) % NX, self.core)

    def z_peer(self, k):
        return self.wide((self.z + k) % NZ, self.x, self.core)

    def y_peer(self, k):
        return {"narrow": (self.n + k) % NY}


def send(src, dst, ssem, rsem, where):
    copy = pltpu.make_async_remote_copy(
        src_ref=src, dst_ref=dst, send_sem=ssem, recv_sem=rsem, device_id=where, device_id_type=MESH
    )
    copy.start()


def wait_bytes(ref, sem):
    pltpu.make_async_copy(ref, ref, sem).wait()


class Cols:
    dtype = BF

    def __init__(self, base, m):
        self.base, self.m, self.rows = base, m, m // NX
        self.xc, self.zc = (m // NX, 1024), (m // NX, 128)

    def x_of(self, q):
        return (ds(self.base + q * self.rows, self.rows), slice(None))

    def z_of(self, q):
        return (slice(None), ds(q * 128, 128))

    def f_z(self, x, z):
        return (ds(self.base + x * self.rows, self.rows), ds(z * 128, 128))


def wide_scratch(lay):
    vm = pltpu.VMEM
    return [
        vm((3,) + lay.xc, lay.dtype),
        vm((3,) + lay.xc, lay.dtype),
        vm(lay.xc, F32),
        vm(lay.xc, lay.dtype),
        vm((7,) + lay.zc, lay.dtype),
        pltpu.SemaphoreType.DMA((4,)),
        pltpu.SemaphoreType.DMA((4,)),
    ]


class WideSum:
    def __init__(self, lay, here, bufs, part, full, extra=None):
        self.lay, self.here, self.part, self.full, self.extra = lay, here, part, full, extra
        self.xsend, self.xrecv, self.own, self.zsend, self.zrecv, self.ss, self.rs = bufs
        self.done = 0

    def x_step(self):
        lay, here = self.lay, self.here
        for k in (2, 1, 3, 0):
            q = lay.x_of((here.x + k) % NX)
            total = self.part[q]
            if self.extra is not None:
                total = total + self.extra[q].astype(F32)
            if k:
                self.xsend[k - 1] = total.astype(lay.dtype)
                send(self.xsend.at[k - 1], self.xrecv.at[k - 1], self.ss.at[0], self.rs.at[0], here.x_peer(k))
            else:
                self.own[...] = total
        self.done = 1

    def z_step(self):
        lay, here = self.lay, self.here
        wait_bytes(self.xrecv, self.rs.at[0])
        total = self.own[...]
        for k in range(3):
            total = total + self.xrecv[k].astype(F32)
        self.own[...] = total
        self.zsend[...] = total.astype(lay.dtype)
        for k in FAR_FIRST:
            send(self.zsend.at[lay.z_of((here.z + k) % NZ)], self.zrecv.at[k - 1],
                 self.ss.at[1], self.rs.at[1], here.z_peer(k))
        self.done = 2

    def z_back(self):
        lay, here = self.lay, self.here
        wait_bytes(self.zrecv, self.rs.at[1])
        total = self.own[lay.z_of(here.z)]
        for k in range(7):
            total = total + self.zrecv[k].astype(F32)
        mine = lay.f_z(here.x, here.z)
        self.full[mine] = total.astype(lay.dtype)
        for k in FAR_FIRST:
            send(self.full.at[mine], self.full.at[mine], self.ss.at[2], self.rs.at[2], here.z_peer(k))
        self.done = 3

    def x_back(self):
        lay, here = self.lay, self.here
        wait_bytes(self.zrecv, self.rs.at[2])
        mine = lay.x_of(here.x)
        for k in (2, 1, 3):
            send(self.full.at[mine], self.full.at[mine], self.ss.at[3], self.rs.at[3], here.x_peer(k))
        self.done = 4

    def finish(self):
        wait_bytes(self.xrecv, self.rs.at[3])
        self.done = 5

    def drain(self):
        for i, ref in enumerate((self.xrecv, self.zrecv, self.zrecv, self.xrecv)):
            if self.done > i:
                wait_bytes(ref, self.ss.at[i])
                if self.done == i + 1:
                    wait_bytes(ref, self.rs.at[i])


GROWS = 3 * H // 2
GZ = GROWS // NZ


def gram_scratch():
    vm = pltpu.VMEM
    return [
        vm((GROWS, H), F32),
        vm((7, GZ, H), F32),
        vm((NX, GZ, H), F32),
        vm((2, GROWS, H), F32),
        pltpu.SemaphoreType.DMA((4,)),
        pltpu.SemaphoreType.DMA((4,)),
    ]


class GramSum:
    def __init__(self, here, bufs):
        self.here = here
        self.part, self.zrecv, self.xall, self.full, self.ss, self.rs = bufs
        self.done = 0

    def z_step(self):
        here = self.here
        for k in FAR_FIRST:
            send(self.part.at[ds(((here.z + k) % NZ) * GZ, GZ)], self.zrecv.at[k - 1],
                 self.ss.at[0], self.rs.at[0], here.z_peer(k))
        self.done = 1

    def x_step(self):
        here = self.here
        wait_bytes(self.zrecv, self.rs.at[0])
        total = self.part[ds(here.z * GZ, GZ)]
        for k in range(7):
            total = total + self.zrecv[k]
        mine = self.xall.at[here.x]
        mine[...] = total
        for k in (2, 1, 3):
            send(mine, mine, self.ss.at[1], self.rs.at[1], here.x_peer(k))
        self.done = 2

    def z_back(self):
        here = self.here
        wait_bytes(self.xall.at[0:3], self.rs.at[1])
        total = self.xall[0]
        for k in range(1, NX):
            total = total + self.xall[k]
        mine = self.full.at[here.core, ds(here.z * GZ, GZ)]
        mine[...] = total
        for k in FAR_FIRST:
            send(mine, mine, self.ss.at[2], self.rs.at[2], here.z_peer(k))
        self.done = 3

    def core_back(self):
        here = self.here
        wait_bytes(self.zrecv, self.rs.at[2])
        mine = self.full.at[here.core]
        send(mine, mine, self.ss.at[3], self.rs.at[3], here.sibling)
        self.done = 4

    def finish(self):
        wait_bytes(self.part, self.rs.at[3])
        self.done = 5

    def drain(self):
        for i, ref in enumerate((self.zrecv, self.xall.at[0:3], self.zrecv, self.part)):
            if self.done > i:
                wait_bytes(ref, self.ss.at[i])
                if self.done == i + 1:
                    wait_bytes(ref, self.rs.at[i])


def narrow_scratch(width):
    return [
        pltpu.VMEM((H, width), BF),
        pltpu.VMEM((7, 16, width), BF),
        pltpu.SemaphoreType.DMA((2,)),
        pltpu.SemaphoreType.DMA((2,)),
    ]


class NarrowSum:
    def __init__(self, here, bufs, full, base=0):
        self.here, self.full, self.base = here, full, base
        self.sendbuf, self.recv, self.ss, self.rs = bufs
        self.done = 0

    def scatter(self, total):
        here = self.here
        self.sendbuf[...] = total.astype(BF)
        for k in FAR_FIRST:
            send(self.sendbuf.at[ds(((here.n + k) % NY) * 16, 16)], self.recv.at[k - 1],
                 self.ss.at[0], self.rs.at[0], here.y_peer(k))
        self.done = 1

    def gather(self):
        here = self.here
        mine = self.sendbuf[ds(here.n * 16, 16)].astype(F32)
        wait_bytes(self.recv, self.rs.at[0])
        for k in range(7):
            mine = mine + self.recv[k].astype(F32)
        at = ds(self.base + here.n * 16, 16)
        self.full[at] = mine.astype(BF)
        for k in FAR_FIRST:
            send(self.full.at[at], self.full.at[at], self.ss.at[1], self.rs.at[1], here.y_peer(k))
        self.done = 2

    def finish(self):
        wait_bytes(self.recv, self.rs.at[1])
        self.done = 3

    def drain(self):
        for i in range(2):
            if self.done > i:
                wait_bytes(self.recv, self.ss.at[i])
                if self.done == i + 1:
                    wait_bytes(self.recv, self.rs.at[i])


NB = 64
GROUP = 16


def thirds(a):
    first = a.astype(BF)
    rest = a - first.astype(F32)
    second = rest.astype(BF)
    return first, second, (rest - second.astype(F32)).astype(BF)


def dot_thirds(a, b):
    a1, a2, a3 = thirds(a)
    b1, b2, b3 = thirds(b)
    return dot(
        jnp.concatenate([a1, a1, a2, a2, a1, a3], axis=1),
        jnp.concatenate([b1, b2, b1, b2, b3, b1], axis=0),
    )


def block_inverse(block):
    shape = (NB, 2 * NB)
    row = lax.broadcasted_iota(jnp.int32, shape, 0)
    col = lax.broadcasted_iota(jnp.int32, shape, 1)
    e = jnp.concatenate([block, jnp.zeros((NB, NB), F32)], axis=1) + (col == row + NB).astype(F32)
    done = []
    for start in range(0, NB, GROUP):
        left = row[:NB - start]
        spread = [jnp.broadcast_to(e[:, start + j:start + j + 1], e.shape) for j in range(GROUP)]
        for p in range(GROUP):
            at = slice(p, p + 1)
            ratio = jnp.where(left > p, spread[p] * (1.0 / spread[p][at]), 0.0)
            for m in range(p + 1, GROUP):
                spread[m] = spread[m] - ratio * spread[m][at]
            e = e - ratio * e[at]
        done.append(e[:GROUP])
        e = e[GROUP:]
    e = jnp.concatenate(done, axis=0)
    diagonal = jnp.sum(jnp.where(row == col, e, 0.0), axis=1, keepdims=True)
    return e[:, NB:] * lax.rsqrt(diagonal)


def inverse_factor(x_ref):
    for b in range(R // NB):
        lo, hi = b * NB, (b + 1) * NB
        m = block_inverse(x_ref[lo:hi, lo:hi])
        rows = dot_thirds(m, x_ref[lo:hi, :])
        lane = lax.broadcasted_iota(jnp.int32, (NB, R), 1)
        pieces = [jnp.zeros((NB, lo), F32)] if lo else []
        pieces.append(m)
        if hi < R:
            pieces.append(jnp.zeros((NB, R - hi), F32))
        out = jnp.where((lane >= lo) & (lane < hi), jnp.concatenate(pieces, axis=1), rows)
        x_ref[lo:hi, :] = out
        if hi < R:
            lane = lax.broadcasted_iota(jnp.int32, (R - hi, R), 1)
            rest = jnp.where((lane >= lo) & (lane < hi), 0.0, x_ref[hi:, :])
            x_ref[hi:, :] = rest - dot_thirds(rows.T[hi:, :], out)
        yield b


CHAIN = [Cols(g * M, M) for g in range(CHAINS)]
WIDE = CHAIN * 4
NARROW = (256, 832, 832, 256)


def body(wt_hbm, u_hbm, s_hbm, basis_ref, proj_ref, scratch, drains):
    here = Place()
    core, n = here.core, here.n
    scratch = list(scratch)

    def take(count):
        got = scratch[:count]
        del scratch[:count]
        return got

    wide_bufs = [take(7) for _ in WIDE]
    narrow_bufs = [take(4) for _ in NARROW]
    gram_bufs = take(6)
    (wt2, u2, s_ref, csend, crecv, part, img1, img2, img3, img4, v_ref, c2, ya, yb, x_ref,
     zbuf, zrecv, zpair, zall, pbuf, precv) = take(21)
    lsem, zss, zrs, psem, qsem = take(5)

    barrier = pltpu.get_barrier_semaphore()
    peers = [here.sibling]
    peers += [here.x_peer(k) for k in range(1, NX)]
    peers += [here.z_peer(k) for k in range(1, NZ)]
    peers += [here.y_peer(k) for k in range(1, NY)]
    for peer in peers:
        pl.semaphore_signal(barrier, inc=1, device_id=peer, device_id_type=MESH)
    loads = [
        pltpu.make_async_copy(wt_hbm, wt2.at[core], lsem.at[0]),
        pltpu.make_async_copy(s_hbm, s_ref, lsem.at[1]),
        pltpu.make_async_copy(u_hbm, u2.at[ds(core * H, H)], lsem.at[2]),
    ]
    for load in loads:
        load.start()
    zbuf[...] = jnp.zeros_like(zbuf)
    for load in loads:
        load.wait()

    def first(c):
        return dot_tn(s_ref[:, ds(c * H, H)], wt2[core])

    csend[...] = first(1 - core).astype(BF)
    pl.semaphore_wait(barrier, len(peers))
    send(csend, crecv, psem.at[0], qsem.at[0], here.sibling)
    mine_u = u2.at[ds(core * H, H)]
    send(wt2.at[core], wt2.at[core], psem.at[1], qsem.at[1], here.sibling)
    send(mine_u, mine_u, psem.at[2], qsem.at[2], here.sibling)
    drains.append(lambda: wait_bytes(csend, psem.at[0]))
    drains.append(lambda: wait_bytes(wt2.at[0], psem.at[1]))
    drains.append(lambda: wait_bytes(u2.at[0:H], psem.at[2]))
    part[...] = first(core)
    wait_bytes(crecv, qsem.at[0])
    yield "start"

    sums = []

    def wide(index, full, parts=part, extra=None):
        got = WideSum(WIDE[index], here, wide_bufs[index], parts, full, extra)
        drains.append(got.drain)
        return got

    def run(chain):
        for step in ROUNDS:
            for s in chain:
                getattr(s, step)()
            yield step

    def narrow(index, full, base=0):
        got = NarrowSum(here, narrow_bufs[index], full, base)
        drains.append(got.drain)
        return got

    yield from run([wide(g, img1, extra=crecv) for g in range(CHAINS)])
    wait_bytes(u2.at[0:H], qsem.at[2])
    n1 = narrow(0, v_ref)
    n1.scatter(dot_nt(img1[...], u2[...]))
    yield "n1s"
    n1.gather()
    yield "n1g"
    n1.finish()
    part[...] = dot(v_ref[...], u2[...])
    yield from run([wide(CHAINS + g, img2) for g in range(CHAINS)])
    wait_bytes(wt2.at[0], qsem.at[1])
    n2 = [narrow(1 + b, c2.at[b]) for b in range(2)]
    for b in range(2):
        n2[b].scatter(dot_nt(img2[...], wt2[b]))
    yield "n2s"
    for b in range(2):
        n2[b].gather()
    yield "n2g"
    n2[0].finish()
    part[...] = dot(c2[0], wt2[0])
    n2[1].finish()
    part[...] += dot(c2[1], wt2[1])
    yield from run([wide(2 * CHAINS + g, img3) for g in range(CHAINS)])
    n3 = narrow(3, ya, core * H)
    n3.scatter(dot_nt(img3[...], u2[...]))
    yield "n3s"
    n3.gather()
    yield "n3g"
    n3.finish()
    mine_y = ya.at[ds(core * H, H)]
    send(mine_y, mine_y, psem.at[3], qsem.at[3], here.sibling)
    drains.append(lambda: wait_bytes(ya.at[0:H], psem.at[3]))
    part[...] = dot(mine_y[...], u2[...])
    last = [wide(3 * CHAINS + g, img4) for g in range(CHAINS)]
    for t in last:
        t.x_step()
    gram = GramSum(here, gram_bufs)
    drains.append(gram.drain)
    wait_bytes(ya.at[0:H], qsem.at[3])
    gram.part[0:H] = dot_nt(mine_y[...], mine_y[...])
    gram.part[H:GROWS] = dot_nt(ya[ds(core * (H // 2), H // 2)], ya[H:R])
    gram.z_step()
    yb[...] = ya[...].astype(F32).T
    yield "gx"
    for t in last:
        t.z_step()
    gram.x_step()
    yield "gz"
    for t in last:
        t.z_back()
    gram.z_back()
    yield "gzb"
    for t in last:
        t.x_back()
    gram.core_back()
    yield "gcb"
    for g in range(CHAINS):
        last[g].finish()
        rows = slice(g * M, (g + 1) * M)
        for b in range(2):
            i = 2 * g + b
            zbuf[b, rows, 0:832] = dot_nt(img4[rows], wt2[b]).astype(BF)
            for k in FAR_FIRST:
                to = (n + k) % NY

                @pl.when(to < 7)
                def _():
                    send(zbuf.at[b, rows, ds(to * 128, 128)], zrecv.at[i, k - 1], zss.at[i], zrs.at[i], here.y_peer(k))

    def drain_z():
        for i in range(2 * CHAINS):

            @pl.when(n < 7)
            def _():
                wait_bytes(zrecv.at[i, 0:6], zss.at[i])

            @pl.when(n == 7)
            def _():
                wait_bytes(zrecv.at[i], zss.at[i])

    drains.append(drain_z)
    gram.finish()
    g = gram.full
    x_ref[0:H, 0:H] = g[0, 0:H]
    x_ref[0:H // 2, H:R] = g[0, H:GROWS]
    x_ref[H // 2:H, H:R] = g[1, H:GROWS]
    x_ref[H:R, 0:H] = jnp.zeros((H, H), F32)
    x_ref[H:R, H:R] = g[1, 0:H]
    yield "gram"
    factor = inverse_factor(x_ref)
    for _ in range(3):
        next(factor)

    @pl.when(n < 7)
    def _():
        for i in range(2 * CHAINS):
            wait_bytes(zrecv.at[i], zrs.at[i])
            rows = slice((i // 2) * M, (i // 2 + 1) * M)
            total = zbuf[i % 2, rows, ds(n * 128, 128)].astype(F32)
            for k in range(7):
                total = total + zrecv[i, k].astype(F32)
            zpair[i % 2, rows] = total.astype(BF)
        to = zall.at[ds(core * H, H)]
        send(zpair.at[1 - core], to, psem.at[8], qsem.at[8], here.sibling)
        to[...] = zpair[core]

    for _ in factor:
        pass
    rr = lax.broadcasted_iota(jnp.int32, (R, R), 0)
    cc = lax.broadcasted_iota(jnp.int32, (R, R), 1)
    inverse = jnp.where(cc <= rr, x_ref[...], 0.0)
    yield "factor"
    high = inverse.astype(BF)
    low = (inverse - high.astype(F32)).astype(BF)

    @pl.when(n < 7)
    def _():
        wait_bytes(zpair.at[0], qsem.at[8])
        pbuf[...] = (dot(high, zall[...]) + dot(low, zall[...])).astype(BF)
        for k in FAR_FIRST:
            send(pbuf.at[ds(((n + k) % NY) * 32, 32)], precv.at[n], psem.at[7], qsem.at[7], here.y_peer(k))
        precv[n] = pbuf[ds(n * 32, 32)]

    rows = yb[ds(core * H + n * 16, 16), :]
    basis_ref[...] = lax.dot_general(
        rows, inverse, (((1,), (1,)), ((), ())), preferred_element_type=F32, precision=lax.Precision.HIGHEST
    ) * math.sqrt(D)

    @pl.when(n < 7)
    def _():
        wait_bytes(precv.at[0:6], qsem.at[7])

    @pl.when(n == 7)
    def _():
        wait_bytes(precv, qsem.at[7])

    for j in range(6):
        proj_ref[:, j * 128:(j + 1) * 128] = precv[j].astype(F32)
    proj_ref[:, 768:832] = precv[6][:, 0:64].astype(F32)

    @pl.when(n < 7)
    def _():
        wait_bytes(zpair.at[0], psem.at[8])
        wait_bytes(precv, psem.at[7])

    yield "end"


def kernel(wt_hbm, u_hbm, s_hbm, basis_ref, proj_ref, *scratch):
    drains = []
    for _ in body(wt_hbm, u_hbm, s_hbm, basis_ref, proj_ref, scratch, drains):
        pass
    for drain in drains:
        drain()


def on_device(weight, whitening, sketch):
    vmem = pl.BlockSpec(memory_space=pltpu.VMEM)
    hbm = pl.BlockSpec(memory_space=pltpu.HBM)
    vm = pltpu.VMEM
    scratch = []
    for lay in WIDE:
        scratch += wide_scratch(lay)
    for width in NARROW:
        scratch += narrow_scratch(width)
    scratch += gram_scratch()
    scratch += [
        vm((2, 832, 1024), BF),
        vm((2 * H, 1024), BF),
        vm((832, R), BF),
        vm((H, 1024), BF),
        vm((H, 1024), BF),
        vm((H, 1024), F32),
        vm((H, 1024), BF),
        vm((H, 1024), BF),
        vm((H, 1024), BF),
        vm((H, 1024), BF),
        vm((H, 2 * H), BF),
        vm((2, H, 832), BF),
        vm((R, 2 * H), BF),
        vm((2 * H, R), F32),
        vm((R, R), F32),
        vm((2, H, 896), BF),
        vm((2 * CHAINS, 7, M, 128), BF),
        vm((2, H, 128), BF),
        vm((R, 128), BF),
        vm((R, 128), BF),
        vm((7, 32, 128), BF),
        pltpu.SemaphoreType.DMA((3,)),
        pltpu.SemaphoreType.DMA((2 * CHAINS,)),
        pltpu.SemaphoreType.DMA((2 * CHAINS,)),
        pltpu.SemaphoreType.DMA((9,)),
        pltpu.SemaphoreType.DMA((9,)),
    ]
    return pl.pallas_call(
        kernel,
        out_shape=(
            jax.ShapeDtypeStruct((16, R), F32),
            jax.ShapeDtypeStruct((32, 832), F32),
        ),
        in_specs=[hbm] * 3,
        out_specs=(vmem, vmem),
        scratch_shapes=scratch,
        compiler_params=pltpu.CompilerParams(
            collective_id=0, has_side_effects=True, vmem_limit_bytes=60 * 1024 * 1024
        ),
        cost_estimate=pl.CostEstimate(flops=2_300_000_000, bytes_accessed=3_000_000, transcendentals=256),
    )(weight.T, whitening, sketch)


def solution(mesh):
    placed = (P("narrow", "wide"), P("wide", "narrow"), P("wide", None))
    return jax.shard_map(
        on_device,
        mesh=mesh,
        in_specs=placed,
        out_specs=(P(("wide", "narrow"), None), P("narrow", "wide")),
        check_vma=False,
    )
```

```python
import math

import jax
import jax.numpy as jnp
from jax import lax
from jax.experimental import pallas as pl
from jax.experimental.pallas import tpu as pltpu
from jax.sharding import PartitionSpec as P

D = 8192
R = 256
H = 128
NX, NZ, NY = 4, 8, 8
CHAINS = 2
XROWS = H // NX
M = XROWS // CHAINS
BF = jnp.bfloat16
F32 = jnp.float32
MESH = pl.DeviceIdType.MESH
FAR_FIRST = (4, 3, 5, 2, 6, 1, 7)
NEAR = (3, 5, 2, 6, 1, 7)
ARRIVAL = (0, 1, 3, 2)


def ds(start, size):
    if isinstance(start, int):
        return pl.ds(start, size)
    return pl.ds(pl.multiple_of(start, size), size)


def dot(a, b):
    return jnp.dot(a, b, preferred_element_type=F32)


def dot_nt(a, b):
    return lax.dot_general(a, b, (((1,), (1,)), ((), ())), preferred_element_type=F32)


def dot_tn(a, b):
    return lax.dot_general(a, b, (((0,), (0,)), ((), ())), preferred_element_type=F32)


class Place:
    def __init__(self):
        w = lax.axis_index("wide")
        self.n = lax.axis_index("narrow")
        self.core = w % 2
        self.x = (w // 2) % NX
        self.z = w // (2 * NX)

    def wide(self, z, x, core):
        return {"wide": (z * NX + x) * 2 + core}

    @property
    def sibling(self):
        return self.wide(self.z, self.x, 1 - self.core)

    def x_peer(self, k):
        return self.wide(self.z, (self.x + k) % NX, self.core)

    def z_peer(self, k):
        return self.wide((self.z + k) % NZ, self.x, self.core)

    def far_peer(self, k):
        return self.wide((self.z + NZ // 2) % NZ, (self.x + k) % NX, self.core)

    def y_peer(self, k):
        return {"narrow": (self.n + k) % NY}


def send(src, dst, ssem, rsem, where):
    copy = pltpu.make_async_remote_copy(
        src_ref=src, dst_ref=dst, send_sem=ssem, recv_sem=rsem, device_id=where, device_id_type=MESH
    )
    copy.start()


def wait_bytes(ref, sem):
    pltpu.make_async_copy(ref, ref, sem).wait()


class Cols:
    dtype, xc, zc = BF, (M, 1024), (M, 128)

    def __init__(self, g):
        self.base = g * M

    def x_of(self, q):
        return (pl.ds(pl.multiple_of(q * XROWS + self.base, M), M), slice(None))

    def z_of(self, q):
        return (slice(None), ds(q * 128, 128))

    def f_z(self, x, z):
        return (pl.ds(pl.multiple_of(x * XROWS + self.base, M), M), ds(z * 128, 128))


def wide_scratch(lay):
    vm = pltpu.VMEM
    return [
        vm((3,) + lay.xc, lay.dtype),
        vm((3,) + lay.xc, lay.dtype),
        vm(lay.xc, F32),
        vm(lay.xc, lay.dtype),
        vm((7,) + lay.zc, lay.dtype),
        vm(lay.zc, lay.dtype),
        vm((NX,) + lay.zc, lay.dtype),
        pltpu.SemaphoreType.DMA((7,)),
        pltpu.SemaphoreType.DMA((13,)),
    ]


class WideSum:
    def __init__(self, lay, here, bufs, part, full, extra=None):
        self.lay, self.here, self.part, self.full, self.extra = lay, here, part, full, extra
        (self.xsend, self.xrecv, self.own, self.zsend, self.zrecv, self.dsend, self.drecv, self.ss, self.rs) = bufs
        self.far = (here.z + NZ // 2) % NZ

    def x_part(self, k):
        lay, here = self.lay, self.here
        q = lay.x_of((here.x + k) % NX)
        total = self.part[q]
        if self.extra is not None:
            total = total + self.extra[q].astype(F32)
        if k:
            self.xsend[k - 1] = total.astype(lay.dtype)
            send(self.xsend.at[k - 1], self.xrecv.at[k - 1], self.ss.at[0], self.rs.at[0], here.x_peer(k))
            direct = self.xsend.at[k - 1].at[lay.z_of(self.far)]
        else:
            self.own[...] = total
            self.dsend[...] = self.own[lay.z_of(self.far)].astype(lay.dtype)
            direct = self.dsend
        send(direct, self.drecv.at[k], self.ss.at[6], self.rs.at[2], here.far_peer(k))

    def x_step(self):
        for k in (2, 1, 3, 0):
            self.x_part(k)

    def z_step(self):
        lay, here = self.lay, self.here
        wait_bytes(self.xrecv, self.rs.at[0])
        total = self.own[...]
        for k in range(3):
            total = total + self.xrecv[k].astype(F32)
        self.own[...] = total
        self.zsend[...] = total.astype(lay.dtype)
        for i, k in enumerate(NEAR):
            send(self.zsend.at[lay.z_of((here.z + k) % NZ)], self.zrecv.at[i],
                 self.ss.at[1], self.rs.at[1], here.z_peer(k))

    def z_back(self):
        lay, here = self.lay, self.here
        wait_bytes(self.zrecv.at[0:6], self.rs.at[1])
        total = self.own[lay.z_of(here.z)]
        for i in range(6):
            total = total + self.zrecv[i].astype(F32)
        wait_bytes(self.drecv, self.rs.at[2])
        for k in range(NX):
            total = total + self.drecv[k].astype(F32)
        mine = lay.f_z(here.x, here.z)
        self.full[mine] = total.astype(lay.dtype)
        mine = self.full.at[mine]
        for k in FAR_FIRST:
            send(mine, mine, self.ss.at[2], self.rs.at[2 + k], here.z_peer(k))
        self.x_forward(0)

    def x_forward(self, k):
        lay, here = self.lay, self.here
        if k:
            wait_bytes(self.zrecv.at[0], self.rs.at[2 + k])
        chunk = self.full.at[lay.f_z(here.x, (here.z + NZ - k) % NZ)]
        for j in (2, 1, 3):
            send(chunk, chunk, self.ss.at[2 + j], self.rs.at[9 + j], here.x_peer(j))

    def wait_x(self, k):
        wait_bytes(self.xrecv.at[0], self.rs.at[9 + k])

    def drain(self):
        wait_bytes(self.xrecv, self.ss.at[0])
        wait_bytes(self.zrecv.at[0:6], self.ss.at[1])
        wait_bytes(self.zrecv, self.ss.at[2])
        for k in range(3):
            wait_bytes(self.xrecv.at[k], self.ss.at[3 + k])
        wait_bytes(self.drecv, self.ss.at[6])


def x_back(chain):
    for k in (1, 7, 2, 6, 3, 5, 4):
        for s in chain:
            s.x_forward(k)


def finish(chain):
    for k in (1, 3, 2):
        for s in chain:
            s.wait_x(k)


GROWS = 3 * H // 2
GZ = GROWS // NZ


def gram_scratch():
    vm = pltpu.VMEM
    return [
        vm((GROWS, H), F32),
        vm((7, GZ, H), F32),
        vm((NX, GZ, H), F32),
        vm((2, GROWS, H), F32),
        pltpu.SemaphoreType.DMA((4,)),
        pltpu.SemaphoreType.DMA((4,)),
    ]


class GramSum:
    def __init__(self, here, bufs):
        self.here = here
        self.part, self.zrecv, self.xall, self.full, self.ss, self.rs = bufs
        self.done = 0

    def z_step(self):
        here = self.here
        for k in FAR_FIRST:
            send(self.part.at[ds(((here.z + k) % NZ) * GZ, GZ)], self.zrecv.at[k - 1],
                 self.ss.at[0], self.rs.at[0], here.z_peer(k))
        self.done = 1

    def x_step(self):
        here = self.here
        wait_bytes(self.zrecv, self.rs.at[0])
        total = self.part[ds(here.z * GZ, GZ)]
        for k in range(7):
            total = total + self.zrecv[k]
        mine = self.xall.at[here.x]
        mine[...] = total
        for k in (2, 1, 3):
            send(mine, mine, self.ss.at[1], self.rs.at[1], here.x_peer(k))
        self.done = 2

    def z_back(self):
        here = self.here
        wait_bytes(self.xall.at[0:3], self.rs.at[1])
        total = self.xall[0]
        for k in range(1, NX):
            total = total + self.xall[k]
        mine = self.full.at[here.core, ds(here.z * GZ, GZ)]
        mine[...] = total
        for k in FAR_FIRST:
            send(mine, mine, self.ss.at[2], self.rs.at[2], here.z_peer(k))
        self.done = 3

    def core_back(self):
        here = self.here
        wait_bytes(self.zrecv, self.rs.at[2])
        mine = self.full.at[here.core]
        send(mine, mine, self.ss.at[3], self.rs.at[3], here.sibling)
        self.done = 4

    def finish(self):
        wait_bytes(self.part, self.rs.at[3])
        self.done = 5

    def drain(self):
        for i, ref in enumerate((self.zrecv, self.xall.at[0:3], self.zrecv, self.part)):
            if self.done > i:
                wait_bytes(ref, self.ss.at[i])
                if self.done == i + 1:
                    wait_bytes(ref, self.rs.at[i])


def narrow_scratch(width):
    return [
        pltpu.VMEM((H, width), BF),
        pltpu.VMEM((7, 16, width), BF),
        pltpu.SemaphoreType.DMA((2,)),
        pltpu.SemaphoreType.DMA((2,)),
    ]


class NarrowSum:
    def __init__(self, here, bufs, full, base=0):
        self.here, self.full, self.base = here, full, base
        self.sendbuf, self.recv, self.ss, self.rs = bufs
        self.done = 0

    def scatter(self, total):
        here = self.here
        self.sendbuf[...] = total.astype(BF)
        for k in FAR_FIRST:
            send(self.sendbuf.at[ds(((here.n + k) % NY) * 16, 16)], self.recv.at[k - 1],
                 self.ss.at[0], self.rs.at[0], here.y_peer(k))
        self.done = 1

    def gather(self):
        here = self.here
        mine = self.sendbuf[ds(here.n * 16, 16)].astype(F32)
        wait_bytes(self.recv, self.rs.at[0])
        for k in range(7):
            mine = mine + self.recv[k].astype(F32)
        at = ds(self.base + here.n * 16, 16)
        self.full[at] = mine.astype(BF)
        for k in FAR_FIRST:
            send(self.full.at[at], self.full.at[at], self.ss.at[1], self.rs.at[1], here.y_peer(k))
        self.done = 2

    def finish(self):
        wait_bytes(self.recv, self.rs.at[1])
        self.done = 3

    def drain(self):
        for i in range(2):
            if self.done > i:
                wait_bytes(self.recv, self.ss.at[i])
                if self.done == i + 1:
                    wait_bytes(self.recv, self.rs.at[i])


def column_scratch():
    return [
        pltpu.VMEM((2, H, 896), BF),
        pltpu.VMEM((NX, 7, 2, XROWS, 128), BF),
        pltpu.SemaphoreType.DMA((NX,)),
        pltpu.SemaphoreType.DMA((NX,)),
    ]


class ColumnSum:
    def __init__(self, here, bufs):
        self.here = here
        self.sendbuf, self.recv, self.ss, self.rs = bufs

    def at(self, k, device):
        q = (self.here.x + NX - k) % NX
        return (slice(None), ds(q * XROWS, XROWS), ds(device * 128, 128))

    def product(self, k, image, wt2):
        here = self.here
        q = ds(((here.x + NX - k) % NX) * XROWS, XROWS)
        for b in range(2):
            self.sendbuf[b, q, 0:832] = dot_nt(image[q], wt2[b]).astype(BF)
        for j in FAR_FIRST:
            to = (here.n + j) % NY

            @pl.when(to < 7)
            def _():
                send(self.sendbuf.at[self.at(k, to)], self.recv.at[k, j - 1],
                     self.ss.at[k], self.rs.at[k], here.y_peer(j))

    def total(self, k):
        wait_bytes(self.recv.at[k], self.rs.at[k])
        total = self.sendbuf[self.at(k, self.here.n)].astype(F32)
        for j in range(7):
            total = total + self.recv[k, j].astype(F32)
        return total

    def drain(self):
        for k in range(NX):
            by_place(self.here, self.recv.at[k], self.ss.at[k])


def by_place(here, seven, sem):
    @pl.when(here.n < 7)
    def _():
        wait_bytes(seven.at[0:6], sem)

    @pl.when(here.n == 7)
    def _():
        wait_bytes(seven, sem)


NB = 64
GROUP = 16


def thirds(a):
    first = a.astype(BF)
    rest = a - first.astype(F32)
    second = rest.astype(BF)
    return first, second, (rest - second.astype(F32)).astype(BF)


def dot_thirds(a, b):
    a1, a2, a3 = thirds(a)
    b1, b2, b3 = thirds(b)
    return dot(
        jnp.concatenate([a1, a1, a2, a2, a1, a3], axis=1),
        jnp.concatenate([b1, b2, b1, b2, b3, b1], axis=0),
    )


def block_inverse(block):
    shape = (NB, 2 * NB)
    row = lax.broadcasted_iota(jnp.int32, shape, 0)
    col = lax.broadcasted_iota(jnp.int32, shape, 1)
    e = jnp.concatenate([block, jnp.zeros((NB, NB), F32)], axis=1) + (col == row + NB).astype(F32)
    done = []
    for start in range(0, NB, GROUP):
        left = row[:NB - start]
        spread = [jnp.broadcast_to(e[:, start + j:start + j + 1], e.shape) for j in range(GROUP)]
        for p in range(GROUP):
            at = slice(p, p + 1)
            ratio = jnp.where(left > p, spread[p] * (1.0 / spread[p][at]), 0.0)
            for m in range(p + 1, GROUP):
                spread[m] = spread[m] - ratio * spread[m][at]
            e = e - ratio * e[at]
        done.append(e[:GROUP])
        e = e[GROUP:]
    e = jnp.concatenate(done, axis=0)
    diagonal = jnp.sum(jnp.where(row == col, e, 0.0), axis=1, keepdims=True)
    return e[:, NB:] * lax.rsqrt(diagonal)


def inverse_factor(x_ref):
    for b in range(R // NB):
        lo, hi = b * NB, (b + 1) * NB
        m = block_inverse(x_ref[lo:hi, lo:hi])
        rows = dot_thirds(m, x_ref[lo:hi, :])
        lane = lax.broadcasted_iota(jnp.int32, (NB, R), 1)
        pieces = [jnp.zeros((NB, lo), F32)] if lo else []
        pieces.append(m)
        if hi < R:
            pieces.append(jnp.zeros((NB, R - hi), F32))
        out = jnp.where((lane >= lo) & (lane < hi), jnp.concatenate(pieces, axis=1), rows)
        x_ref[lo:hi, :] = out
        if hi < R:
            lane = lax.broadcasted_iota(jnp.int32, (R - hi, R), 1)
            rest = jnp.where((lane >= lo) & (lane < hi), 0.0, x_ref[hi:, :])
            x_ref[hi:, :] = rest - dot_thirds(rows.T[hi:, :], out)
        yield b


CHAIN = [Cols(g) for g in range(CHAINS)]
WIDE = CHAIN * 4
NARROW = (256, 256)


def body(wt_hbm, u_hbm, s_hbm, basis_ref, proj_ref, scratch, drains):
    here = Place()
    core, n = here.core, here.n
    scratch = list(scratch)

    def take(count):
        got = scratch[:count]
        del scratch[:count]
        return got

    wide_bufs = [take(9) for _ in WIDE]
    narrow_bufs = [take(4) for _ in NARROW]
    gram_bufs = take(6)
    column_bufs = [take(4) for _ in range(2)]
    (wt2, u2, s_ref, csend, crecv, part, img1, img2, img3, img4, v_ref, c2, ya, yb, x_ref,
     zpair, zall, pbuf, precv) = take(19)
    lsem, css, crs, psem, qsem = take(5)

    barrier = pltpu.get_barrier_semaphore()
    peers = [here.sibling]
    peers += [here.x_peer(k) for k in range(1, NX)]
    peers += [here.z_peer(k) for k in range(1, NZ)]
    peers += [here.far_peer(k) for k in range(1, NX)]
    peers += [here.y_peer(k) for k in range(1, NY)]
    for peer in peers:
        pl.semaphore_signal(barrier, inc=1, device_id=peer, device_id_type=MESH)
    loads = [
        pltpu.make_async_copy(wt_hbm, wt2.at[core], lsem.at[0]),
        pltpu.make_async_copy(s_hbm, s_ref, lsem.at[1]),
        pltpu.make_async_copy(u_hbm, u2.at[ds(core * H, H)], lsem.at[2]),
    ]
    for load in loads:
        load.start()
    columns = [ColumnSum(here, bufs) for bufs in column_bufs]
    for c in columns:
        c.sendbuf[...] = jnp.zeros_like(c.sendbuf)
    for load in loads:
        load.wait()

    def first(c):
        return dot_tn(s_ref[:, ds(c * H, H)], wt2[core])

    csend[...] = first(1 - core).astype(BF)
    pl.semaphore_wait(barrier, len(peers))
    send(csend, crecv, psem.at[0], qsem.at[0], here.sibling)
    mine_u = u2.at[ds(core * H, H)]
    send(wt2.at[core], wt2.at[core], psem.at[1], qsem.at[1], here.sibling)
    send(mine_u, mine_u, psem.at[2], qsem.at[2], here.sibling)
    drains.append(lambda: wait_bytes(csend, psem.at[0]))
    drains.append(lambda: wait_bytes(wt2.at[0], psem.at[1]))
    drains.append(lambda: wait_bytes(u2.at[0:H], psem.at[2]))
    part[...] = first(core)
    wait_bytes(crecv, qsem.at[0])

    sums = []

    def wide(index, full, parts=part, extra=None):
        got = WideSum(WIDE[index], here, wide_bufs[index], parts, full, extra)
        drains.append(got.drain)
        return got

    def run(chain, scattered=False):
        if not scattered:
            for s in chain:
                s.x_step()
        for s in chain:
            s.z_step()
        for s in chain:
            s.z_back()
        x_back(chain)

    def narrow(index, full, base=0):
        got = NarrowSum(here, narrow_bufs[index], full, base)
        drains.append(got.drain)
        return got

    first_image = [wide(g, img1, extra=crecv) for g in range(CHAINS)]
    run(first_image)
    finish(first_image)
    wait_bytes(u2.at[0:H], qsem.at[2])
    n1 = narrow(0, v_ref)
    n1.scatter(dot_nt(img1[...], u2[...]))
    n1.gather()
    n1.finish()
    part[...] = dot(v_ref[...], u2[...])
    back = [wide(CHAINS + g, img2) for g in range(CHAINS)]
    run(back)
    wait_bytes(wt2.at[0], qsem.at[1])
    feature = columns[0]
    drains.append(feature.drain)
    for k in ARRIVAL:
        if k:
            for s in back:
                s.wait_x(k)
        feature.product(k, img2, wt2)
    for k in ARRIVAL:

        @pl.when(n < 7)
        def _():
            mine = feature.at(k, n)
            c2[mine] = feature.total(k).astype(BF)
            for j in FAR_FIRST:
                send(c2.at[mine], c2.at[mine], css.at[k], crs.at[k], here.y_peer(j))

    def drain_c():
        @pl.when(n < 7)
        def _():
            for k in range(NX):
                wait_bytes(feature.recv.at[k], css.at[k])

    drains.append(drain_c)
    second = [wide(2 * CHAINS + g, img3) for g in range(CHAINS)]
    for k in ARRIVAL:
        by_place(here, feature.recv.at[k], crs.at[k])
        q = ds(((here.x + NX - k) % NX) * XROWS, XROWS)
        part[q] = dot(c2[0, q, 0:832], wt2[0]) + dot(c2[1, q, 0:832], wt2[1])
        for s in second:
            s.x_part((NX - k) % NX)
    run(second, scattered=True)
    finish(second)
    n3 = narrow(1, ya, core * H)
    n3.scatter(dot_nt(img3[...], u2[...]))
    n3.gather()
    n3.finish()
    mine_y = ya.at[ds(core * H, H)]
    send(mine_y, mine_y, psem.at[3], qsem.at[3], here.sibling)
    drains.append(lambda: wait_bytes(ya.at[0:H], psem.at[3]))
    part[...] = dot(mine_y[...], u2[...])
    last = [wide(3 * CHAINS + g, img4) for g in range(CHAINS)]
    for t in last:
        t.x_step()
    gram = GramSum(here, gram_bufs)
    drains.append(gram.drain)
    wait_bytes(ya.at[0:H], qsem.at[3])
    gram.part[0:H] = dot_nt(mine_y[...], mine_y[...])
    gram.part[H:GROWS] = dot_nt(ya[ds(core * (H // 2), H // 2)], ya[H:R])
    gram.z_step()
    yb[...] = ya[...].astype(F32).T
    for t in last:
        t.z_step()
    gram.x_step()
    for t in last:
        t.z_back()
    gram.z_back()
    x_back(last)
    z = columns[1]
    drains.append(z.drain)
    z.product(0, img4, wt2)
    gram.core_back()
    for k in ARRIVAL[1:]:
        for t in last:
            t.wait_x(k)
        z.product(k, img4, wt2)
    gram.finish()
    g = gram.full
    x_ref[0:H, 0:H] = g[0, 0:H]
    x_ref[0:H // 2, H:R] = g[0, H:GROWS]
    x_ref[H // 2:H, H:R] = g[1, H:GROWS]
    x_ref[H:R, 0:H] = jnp.zeros((H, H), F32)
    x_ref[H:R, H:R] = g[1, 0:H]
    factor = inverse_factor(x_ref)
    for _ in range(3):
        next(factor)

    @pl.when(n < 7)
    def _():
        for k in ARRIVAL:
            q = ds(((here.x + NX - k) % NX) * XROWS, XROWS)
            zpair[:, q] = z.total(k).astype(BF)
        to = zall.at[ds(core * H, H)]
        send(zpair.at[1 - core], to, psem.at[8], qsem.at[8], here.sibling)
        to[...] = zpair[core]

    for _ in factor:
        pass
    rr = lax.broadcasted_iota(jnp.int32, (R, R), 0)
    cc = lax.broadcasted_iota(jnp.int32, (R, R), 1)
    inverse = jnp.where(cc <= rr, x_ref[...], 0.0)
    high = inverse.astype(BF)
    low = (inverse - high.astype(F32)).astype(BF)

    @pl.when(n < 7)
    def _():
        wait_bytes(zpair.at[0], qsem.at[8])
        pbuf[...] = (dot(high, zall[...]) + dot(low, zall[...])).astype(BF)
        for k in FAR_FIRST:
            send(pbuf.at[ds(((n + k) % NY) * 32, 32)], precv.at[n], psem.at[7], qsem.at[7], here.y_peer(k))
        precv[n] = pbuf[ds(n * 32, 32)]

    rows = yb[ds(core * H + n * 16, 16), :]
    basis_ref[...] = lax.dot_general(
        rows, inverse, (((1,), (1,)), ((), ())), preferred_element_type=F32, precision=lax.Precision.HIGHEST
    ) * math.sqrt(D)
    by_place(here, precv, qsem.at[7])

    for j in range(6):
        proj_ref[:, j * 128:(j + 1) * 128] = precv[j].astype(F32)
    proj_ref[:, 768:832] = precv[6][:, 0:64].astype(F32)

    @pl.when(n < 7)
    def _():
        wait_bytes(zpair.at[0], psem.at[8])
        wait_bytes(precv, psem.at[7])


def kernel(wt_hbm, u_hbm, s_hbm, basis_ref, proj_ref, *scratch):
    drains = []
    body(wt_hbm, u_hbm, s_hbm, basis_ref, proj_ref, scratch, drains)
    for drain in drains:
        drain()


def on_device(weight, whitening, sketch):
    vmem = pl.BlockSpec(memory_space=pltpu.VMEM)
    hbm = pl.BlockSpec(memory_space=pltpu.HBM)
    vm = pltpu.VMEM
    scratch = []
    for lay in WIDE:
        scratch += wide_scratch(lay)
    for width in NARROW:
        scratch += narrow_scratch(width)
    scratch += gram_scratch() + column_scratch() + column_scratch()
    scratch += [
        vm((2, 832, 1024), BF),
        vm((2 * H, 1024), BF),
        vm((832, R), BF),
        vm((H, 1024), BF),
        vm((H, 1024), BF),
        vm((H, 1024), F32),
        vm((H, 1024), BF),
        vm((H, 1024), BF),
        vm((H, 1024), BF),
        vm((H, 1024), BF),
        vm((H, 2 * H), BF),
        vm((2, H, 896), BF),
        vm((R, 2 * H), BF),
        vm((2 * H, R), F32),
        vm((R, R), F32),
        vm((2, H, 128), BF),
        vm((R, 128), BF),
        vm((R, 128), BF),
        vm((7, 32, 128), BF),
        pltpu.SemaphoreType.DMA((3,)),
        pltpu.SemaphoreType.DMA((NX,)),
        pltpu.SemaphoreType.DMA((NX,)),
        pltpu.SemaphoreType.DMA((9,)),
        pltpu.SemaphoreType.DMA((9,)),
    ]
    return pl.pallas_call(
        kernel,
        out_shape=(
            jax.ShapeDtypeStruct((16, R), F32),
            jax.ShapeDtypeStruct((32, 832), F32),
        ),
        in_specs=[hbm] * 3,
        out_specs=(vmem, vmem),
        scratch_shapes=scratch,
        compiler_params=pltpu.CompilerParams(
            collective_id=0, has_side_effects=True, vmem_limit_bytes=60 * 1024 * 1024
        ),
        cost_estimate=pl.CostEstimate(flops=2_300_000_000, bytes_accessed=3_000_000, transcendentals=256),
    )(weight.T, whitening, sketch)


def solution(mesh):
    placed = (P("narrow", "wide"), P("wide", "narrow"), P("wide", None))
    return jax.shard_map(
        on_device,
        mesh=mesh,
        in_specs=placed,
        out_specs=(P(("wide", "narrow"), None), P("narrow", "wide")),
        check_vma=False,
    )
```

```python
import math

import jax
import jax.numpy as jnp
from jax import lax
from jax.experimental import pallas as pl
from jax.experimental.pallas import tpu as pltpu
from jax.sharding import PartitionSpec as P

D = 8192
R = 256
H = 128
NX, NZ, NY = 4, 8, 8
CHAINS = 2
XROWS = H // NX
M = XROWS // CHAINS
BF = jnp.bfloat16
F32 = jnp.float32
MESH = pl.DeviceIdType.MESH
FAR_FIRST = (4, 3, 5, 2, 6, 1, 7)
NEAR = (3, 5, 2, 6, 1, 7)
ARRIVAL = (0, 1, 3, 2)


def ds(start, size):
    if isinstance(start, int):
        return pl.ds(start, size)
    return pl.ds(pl.multiple_of(start, size), size)


def dot(a, b):
    return jnp.dot(a, b, preferred_element_type=F32)


def dot_nt(a, b):
    return lax.dot_general(a, b, (((1,), (1,)), ((), ())), preferred_element_type=F32)


def dot_tn(a, b):
    return lax.dot_general(a, b, (((0,), (0,)), ((), ())), preferred_element_type=F32)


class Place:
    def __init__(self):
        w = lax.axis_index("wide")
        self.n = lax.axis_index("narrow")
        self.core = w % 2
        self.x = (w // 2) % NX
        self.z = w // (2 * NX)

    def wide(self, z, x, core):
        return {"wide": (z * NX + x) * 2 + core}

    @property
    def sibling(self):
        return self.wide(self.z, self.x, 1 - self.core)

    def x_peer(self, k):
        return self.wide(self.z, (self.x + k) % NX, self.core)

    def z_peer(self, k):
        return self.wide((self.z + k) % NZ, self.x, self.core)

    def far_peer(self, k):
        return self.wide((self.z + NZ // 2) % NZ, (self.x + k) % NX, self.core)

    def y_peer(self, k):
        return {"narrow": (self.n + k) % NY}


def send(src, dst, ssem, rsem, where):
    copy = pltpu.make_async_remote_copy(
        src_ref=src, dst_ref=dst, send_sem=ssem, recv_sem=rsem, device_id=where, device_id_type=MESH
    )
    copy.start()


def wait_bytes(ref, sem):
    pltpu.make_async_copy(ref, ref, sem).wait()


class Cols:
    dtype, xc, zc = BF, (M, 1024), (M, 128)

    def __init__(self, g):
        self.base = g * M

    def x_of(self, q):
        return (pl.ds(pl.multiple_of(q * XROWS + self.base, M), M), slice(None))

    def z_of(self, q):
        return (slice(None), ds(q * 128, 128))

    def f_z(self, x, z):
        return (pl.ds(pl.multiple_of(x * XROWS + self.base, M), M), ds(z * 128, 128))


def wide_scratch(lay):
    vm = pltpu.VMEM
    return [
        vm((3,) + lay.xc, lay.dtype),
        vm((3,) + lay.xc, lay.dtype),
        vm(lay.xc, F32),
        vm(lay.xc, lay.dtype),
        vm((7,) + lay.zc, lay.dtype),
        vm(lay.zc, lay.dtype),
        vm((NX,) + lay.zc, lay.dtype),
        pltpu.SemaphoreType.DMA((7,)),
        pltpu.SemaphoreType.DMA((13,)),
    ]


class WideSum:
    def __init__(self, lay, here, bufs, part, full, extra=None):
        self.lay, self.here, self.part, self.full, self.extra = lay, here, part, full, extra
        (self.xsend, self.xrecv, self.own, self.zsend, self.zrecv, self.dsend, self.drecv, self.ss, self.rs) = bufs
        self.far = (here.z + NZ // 2) % NZ

    def x_part(self, k):
        lay, here = self.lay, self.here
        q = lay.x_of((here.x + k) % NX)
        total = self.part[q]
        if self.extra is not None:
            total = total + self.extra[q].astype(F32)
        if k:
            self.xsend[k - 1] = total.astype(lay.dtype)
            send(self.xsend.at[k - 1], self.xrecv.at[k - 1], self.ss.at[0], self.rs.at[0], here.x_peer(k))
            direct = self.xsend.at[k - 1].at[lay.z_of(self.far)]
        else:
            self.own[...] = total
            self.dsend[...] = self.own[lay.z_of(self.far)].astype(lay.dtype)
            direct = self.dsend
        send(direct, self.drecv.at[k], self.ss.at[6], self.rs.at[2], here.far_peer(k))

    def x_step(self):
        for k in (2, 1, 3, 0):
            self.x_part(k)

    def z_step(self):
        lay, here = self.lay, self.here
        wait_bytes(self.xrecv, self.rs.at[0])
        total = self.own[...]
        for k in range(3):
            total = total + self.xrecv[k].astype(F32)
        self.own[...] = total
        self.zsend[...] = total.astype(lay.dtype)
        for i, k in enumerate(NEAR):
            send(self.zsend.at[lay.z_of((here.z + k) % NZ)], self.zrecv.at[i],
                 self.ss.at[1], self.rs.at[1], here.z_peer(k))

    def z_back(self):
        lay, here = self.lay, self.here
        wait_bytes(self.zrecv.at[0:6], self.rs.at[1])
        total = self.own[lay.z_of(here.z)]
        for i in range(6):
            total = total + self.zrecv[i].astype(F32)
        wait_bytes(self.drecv, self.rs.at[2])
        for k in range(NX):
            total = total + self.drecv[k].astype(F32)
        mine = lay.f_z(here.x, here.z)
        self.full[mine] = total.astype(lay.dtype)
        mine = self.full.at[mine]
        for k in FAR_FIRST:
            send(mine, mine, self.ss.at[2], self.rs.at[2 + k], here.z_peer(k))
        self.x_forward(0)

    def x_forward(self, k):
        lay, here = self.lay, self.here
        if k:
            wait_bytes(self.zrecv.at[0], self.rs.at[2 + k])
        chunk = self.full.at[lay.f_z(here.x, (here.z + NZ - k) % NZ)]
        for j in (2, 1, 3):
            send(chunk, chunk, self.ss.at[2 + j], self.rs.at[9 + j], here.x_peer(j))

    def wait_x(self, k):
        wait_bytes(self.xrecv.at[0], self.rs.at[9 + k])

    def drain(self):
        wait_bytes(self.xrecv, self.ss.at[0])
        wait_bytes(self.zrecv.at[0:6], self.ss.at[1])
        wait_bytes(self.zrecv, self.ss.at[2])
        for k in range(3):
            wait_bytes(self.xrecv.at[k], self.ss.at[3 + k])
        wait_bytes(self.drecv, self.ss.at[6])


def x_back(chain):
    for k in (1, 7, 2, 6, 3, 5, 4):
        for s in chain:
            s.x_forward(k)


def finish(chain):
    for k in (1, 3, 2):
        for s in chain:
            s.wait_x(k)


GROWS = 3 * H // 2
GZ = GROWS // NZ


def gram_scratch():
    vm = pltpu.VMEM
    return [
        vm((GROWS, H), F32),
        vm((7, GZ, H), F32),
        vm((NX, GZ, H), F32),
        vm((2, GROWS, H), F32),
        pltpu.SemaphoreType.DMA((4,)),
        pltpu.SemaphoreType.DMA((4,)),
    ]


class GramSum:
    def __init__(self, here, bufs):
        self.here = here
        self.part, self.zrecv, self.xall, self.full, self.ss, self.rs = bufs
        self.done = 0

    def z_step(self):
        here = self.here
        for k in FAR_FIRST:
            send(self.part.at[ds(((here.z + k) % NZ) * GZ, GZ)], self.zrecv.at[k - 1],
                 self.ss.at[0], self.rs.at[0], here.z_peer(k))
        self.done = 1

    def x_step(self):
        here = self.here
        wait_bytes(self.zrecv, self.rs.at[0])
        total = self.part[ds(here.z * GZ, GZ)]
        for k in range(7):
            total = total + self.zrecv[k]
        mine = self.xall.at[here.x]
        mine[...] = total
        for k in (2, 1, 3):
            send(mine, mine, self.ss.at[1], self.rs.at[1], here.x_peer(k))
        self.done = 2

    def z_back(self):
        here = self.here
        wait_bytes(self.xall.at[0:3], self.rs.at[1])
        total = self.xall[0]
        for k in range(1, NX):
            total = total + self.xall[k]
        mine = self.full.at[here.core, ds(here.z * GZ, GZ)]
        mine[...] = total
        for k in FAR_FIRST:
            send(mine, mine, self.ss.at[2], self.rs.at[2], here.z_peer(k))
        self.done = 3

    def core_back(self):
        here = self.here
        wait_bytes(self.zrecv, self.rs.at[2])
        mine = self.full.at[here.core]
        send(mine, mine, self.ss.at[3], self.rs.at[3], here.sibling)
        self.done = 4

    def finish(self):
        wait_bytes(self.part, self.rs.at[3])
        self.done = 5

    def drain(self):
        for i, ref in enumerate((self.zrecv, self.xall.at[0:3], self.zrecv, self.part)):
            if self.done > i:
                wait_bytes(ref, self.ss.at[i])
                if self.done == i + 1:
                    wait_bytes(ref, self.rs.at[i])


def narrow_scratch(width):
    return [
        pltpu.VMEM((H, width), BF),
        pltpu.VMEM((7, 16, width), BF),
        pltpu.SemaphoreType.DMA((2,)),
        pltpu.SemaphoreType.DMA((2,)),
    ]


class NarrowSum:
    def __init__(self, here, bufs, full, base=0):
        self.here, self.full, self.base = here, full, base
        self.sendbuf, self.recv, self.ss, self.rs = bufs
        self.done = 0

    def scatter(self, total):
        here = self.here
        self.sendbuf[...] = total.astype(BF)
        for k in FAR_FIRST:
            send(self.sendbuf.at[ds(((here.n + k) % NY) * 16, 16)], self.recv.at[k - 1],
                 self.ss.at[0], self.rs.at[0], here.y_peer(k))
        self.done = 1

    def gather(self):
        here = self.here
        mine = self.sendbuf[ds(here.n * 16, 16)].astype(F32)
        wait_bytes(self.recv, self.rs.at[0])
        for k in range(7):
            mine = mine + self.recv[k].astype(F32)
        at = ds(self.base + here.n * 16, 16)
        self.full[at] = mine.astype(BF)
        for k in FAR_FIRST:
            send(self.full.at[at], self.full.at[at], self.ss.at[1], self.rs.at[1], here.y_peer(k))
        self.done = 2

    def finish(self):
        wait_bytes(self.recv, self.rs.at[1])
        self.done = 3

    def drain(self):
        for i in range(2):
            if self.done > i:
                wait_bytes(self.recv, self.ss.at[i])
                if self.done == i + 1:
                    wait_bytes(self.recv, self.rs.at[i])


def column_scratch():
    return [
        pltpu.VMEM((2, H, 896), BF),
        pltpu.VMEM((NX, 7, 2, XROWS, 128), BF),
        pltpu.SemaphoreType.DMA((NX,)),
        pltpu.SemaphoreType.DMA((NX,)),
    ]


class ColumnSum:
    def __init__(self, here, bufs, turns):
        self.here, self.turns = here, turns
        self.sendbuf, self.recv, self.ss, self.rs = bufs

    def tile(self, k, device):
        if not self.turns:
            return device
        q = (self.here.x + NX - k) % NX
        return (device + NY - 2 * q) % NY

    def at(self, k, device):
        q = (self.here.x + NX - k) % NX
        return (slice(None), ds(q * XROWS, XROWS), ds(self.tile(k, device) * 128, 128))

    def by_place(self, k, seven, sem):
        tile = self.tile(k, self.here.n)

        @pl.when(tile < 7)
        def _():
            wait_bytes(seven.at[0:6], sem)

        @pl.when(tile == 7)
        def _():
            wait_bytes(seven, sem)

    def product(self, k, image, wt2):
        here = self.here
        q = ds(((here.x + NX - k) % NX) * XROWS, XROWS)
        for b in range(2):
            self.sendbuf[b, q, 0:832] = dot_nt(image[q], wt2[b]).astype(BF)
        for j in FAR_FIRST:
            to = (here.n + j) % NY

            @pl.when(self.tile(k, to) < 7)
            def _():
                send(self.sendbuf.at[self.at(k, to)], self.recv.at[k, j - 1],
                     self.ss.at[k], self.rs.at[k], here.y_peer(j))

    def total(self, k):
        wait_bytes(self.recv.at[k], self.rs.at[k])
        total = self.sendbuf[self.at(k, self.here.n)].astype(F32)
        for j in range(7):
            total = total + self.recv[k, j].astype(F32)
        return total

    def drain(self):
        for k in range(NX):
            self.by_place(k, self.recv.at[k], self.ss.at[k])


NB = 64
GROUP = 16


def thirds(a):
    first = a.astype(BF)
    rest = a - first.astype(F32)
    second = rest.astype(BF)
    return first, second, (rest - second.astype(F32)).astype(BF)


def dot_thirds(a, b):
    a1, a2, a3 = thirds(a)
    b1, b2, b3 = thirds(b)
    return dot(
        jnp.concatenate([a1, a1, a2, a2, a1, a3], axis=1),
        jnp.concatenate([b1, b2, b1, b2, b3, b1], axis=0),
    )


def block_inverse(block):
    shape = (NB, 2 * NB)
    row = lax.broadcasted_iota(jnp.int32, shape, 0)
    col = lax.broadcasted_iota(jnp.int32, shape, 1)
    e = jnp.concatenate([block, jnp.zeros((NB, NB), F32)], axis=1) + (col == row + NB).astype(F32)
    done = []
    for start in range(0, NB, GROUP):
        left = row[:NB - start]
        spread = [jnp.broadcast_to(e[:, start + j:start + j + 1], e.shape) for j in range(GROUP)]
        for p in range(GROUP):
            at = slice(p, p + 1)
            ratio = jnp.where(left > p, spread[p] * (1.0 / spread[p][at]), 0.0)
            for m in range(p + 1, GROUP):
                spread[m] = spread[m] - ratio * spread[m][at]
            e = e - ratio * e[at]
        done.append(e[:GROUP])
        e = e[GROUP:]
    e = jnp.concatenate(done, axis=0)
    diagonal = jnp.sum(jnp.where(row == col, e, 0.0), axis=1, keepdims=True)
    return e[:, NB:] * lax.rsqrt(diagonal)


def inverse_factor(x_ref):
    for b in range(R // NB):
        lo, hi = b * NB, (b + 1) * NB
        m = block_inverse(x_ref[lo:hi, lo:hi])
        rows = dot_thirds(m, x_ref[lo:hi, :])
        lane = lax.broadcasted_iota(jnp.int32, (NB, R), 1)
        pieces = [jnp.zeros((NB, lo), F32)] if lo else []
        pieces.append(m)
        if hi < R:
            pieces.append(jnp.zeros((NB, R - hi), F32))
        out = jnp.where((lane >= lo) & (lane < hi), jnp.concatenate(pieces, axis=1), rows)
        x_ref[lo:hi, :] = out
        if hi < R:
            lane = lax.broadcasted_iota(jnp.int32, (R - hi, R), 1)
            rest = jnp.where((lane >= lo) & (lane < hi), 0.0, x_ref[hi:, :])
            x_ref[hi:, :] = rest - dot_thirds(rows.T[hi:, :], out)
        yield b


CHAIN = [Cols(g) for g in range(CHAINS)]
WIDE = CHAIN * 4
NARROW = (256, 256)


def body(wt_hbm, u_hbm, s_hbm, basis_ref, proj_ref, scratch, drains):
    here = Place()
    core, n = here.core, here.n
    scratch = list(scratch)

    def take(count):
        got = scratch[:count]
        del scratch[:count]
        return got

    wide_bufs = [take(9) for _ in WIDE]
    narrow_bufs = [take(4) for _ in NARROW]
    gram_bufs = take(6)
    column_bufs = [take(4) for _ in range(2)]
    (wt2, u2, s_ref, csend, crecv, part, img1, img2, img3, img4, v_ref, c2, ya, yb, x_ref,
     zpair, zall, pbuf, precv) = take(19)
    lsem, css, crs, psem, qsem = take(5)

    barrier = pltpu.get_barrier_semaphore()
    peers = [here.sibling]
    peers += [here.x_peer(k) for k in range(1, NX)]
    peers += [here.z_peer(k) for k in range(1, NZ)]
    peers += [here.far_peer(k) for k in range(1, NX)]
    peers += [here.y_peer(k) for k in range(1, NY)]
    for peer in peers:
        pl.semaphore_signal(barrier, inc=1, device_id=peer, device_id_type=MESH)
    loads = [
        pltpu.make_async_copy(wt_hbm, wt2.at[core], lsem.at[0]),
        pltpu.make_async_copy(s_hbm, s_ref, lsem.at[1]),
        pltpu.make_async_copy(u_hbm, u2.at[ds(core * H, H)], lsem.at[2]),
    ]
    for load in loads:
        load.start()
    columns = [ColumnSum(here, bufs, turns) for bufs, turns in zip(column_bufs, (True, False))]
    for c in columns:
        c.sendbuf[...] = jnp.zeros_like(c.sendbuf)
    for load in loads:
        load.wait()

    def first(c):
        return dot_tn(s_ref[:, ds(c * H, H)], wt2[core])

    csend[...] = first(1 - core).astype(BF)
    pl.semaphore_wait(barrier, len(peers))
    send(csend, crecv, psem.at[0], qsem.at[0], here.sibling)
    mine_u = u2.at[ds(core * H, H)]
    send(wt2.at[core], wt2.at[core], psem.at[1], qsem.at[1], here.sibling)
    send(mine_u, mine_u, psem.at[2], qsem.at[2], here.sibling)
    drains.append(lambda: wait_bytes(csend, psem.at[0]))
    drains.append(lambda: wait_bytes(wt2.at[0], psem.at[1]))
    drains.append(lambda: wait_bytes(u2.at[0:H], psem.at[2]))
    part[...] = first(core)
    wait_bytes(crecv, qsem.at[0])

    sums = []

    def wide(index, full, parts=part, extra=None):
        got = WideSum(WIDE[index], here, wide_bufs[index], parts, full, extra)
        drains.append(got.drain)
        return got

    def run(chain, scattered=False):
        if not scattered:
            for s in chain:
                s.x_step()
        for s in chain:
            s.z_step()
        for s in chain:
            s.z_back()
        x_back(chain)

    def narrow(index, full, base=0):
        got = NarrowSum(here, narrow_bufs[index], full, base)
        drains.append(got.drain)
        return got

    first_image = [wide(g, img1, extra=crecv) for g in range(CHAINS)]
    run(first_image)
    finish(first_image)
    wait_bytes(u2.at[0:H], qsem.at[2])
    n1 = narrow(0, v_ref)
    n1.scatter(dot_nt(img1[...], u2[...]))
    n1.gather()
    n1.finish()
    part[...] = dot(v_ref[...], u2[...])
    back = [wide(CHAINS + g, img2) for g in range(CHAINS)]
    run(back)
    wait_bytes(wt2.at[0], qsem.at[1])
    feature = columns[0]
    drains.append(feature.drain)
    for k in ARRIVAL:
        if k:
            for s in back:
                s.wait_x(k)
        feature.product(k, img2, wt2)
    for k in ARRIVAL:

        @pl.when(feature.tile(k, n) < 7)
        def _():
            mine = feature.at(k, n)
            c2[mine] = feature.total(k).astype(BF)
            for j in FAR_FIRST:
                send(c2.at[mine], c2.at[mine], css.at[k], crs.at[k], here.y_peer(j))

    def drain_c():
        for k in range(NX):

            @pl.when(feature.tile(k, n) < 7)
            def _():
                wait_bytes(feature.recv.at[k], css.at[k])

    drains.append(drain_c)
    second = [wide(2 * CHAINS + g, img3) for g in range(CHAINS)]
    for k in ARRIVAL:
        feature.by_place(k, feature.recv.at[k], crs.at[k])
        q = ds(((here.x + NX - k) % NX) * XROWS, XROWS)
        part[q] = dot(c2[0, q, 0:832], wt2[0]) + dot(c2[1, q, 0:832], wt2[1])
        for s in second:
            s.x_part((NX - k) % NX)
    run(second, scattered=True)
    finish(second)
    n3 = narrow(1, ya, core * H)
    n3.scatter(dot_nt(img3[...], u2[...]))
    n3.gather()
    n3.finish()
    mine_y = ya.at[ds(core * H, H)]
    send(mine_y, mine_y, psem.at[3], qsem.at[3], here.sibling)
    drains.append(lambda: wait_bytes(ya.at[0:H], psem.at[3]))
    part[...] = dot(mine_y[...], u2[...])
    last = [wide(3 * CHAINS + g, img4) for g in range(CHAINS)]
    for t in last:
        t.x_step()
    gram = GramSum(here, gram_bufs)
    drains.append(gram.drain)
    wait_bytes(ya.at[0:H], qsem.at[3])
    gram.part[0:H] = dot_nt(mine_y[...], mine_y[...])
    gram.part[H:GROWS] = dot_nt(ya[ds(core * (H // 2), H // 2)], ya[H:R])
    gram.z_step()
    yb[...] = ya[...].astype(F32).T
    for t in last:
        t.z_step()
    gram.x_step()
    for t in last:
        t.z_back()
    gram.z_back()
    x_back(last)
    z = columns[1]
    drains.append(z.drain)
    z.product(0, img4, wt2)
    gram.core_back()
    for k in ARRIVAL[1:]:
        for t in last:
            t.wait_x(k)
        z.product(k, img4, wt2)
    gram.finish()
    g = gram.full
    x_ref[0:H, 0:H] = g[0, 0:H]
    x_ref[0:H // 2, H:R] = g[0, H:GROWS]
    x_ref[H // 2:H, H:R] = g[1, H:GROWS]
    x_ref[H:R, 0:H] = jnp.zeros((H, H), F32)
    x_ref[H:R, H:R] = g[1, 0:H]
    factor = inverse_factor(x_ref)
    for _ in range(3):
        next(factor)

    @pl.when(n < 7)
    def _():
        for k in ARRIVAL:
            q = ds(((here.x + NX - k) % NX) * XROWS, XROWS)
            zpair[:, q] = z.total(k).astype(BF)
        to = zall.at[ds(core * H, H)]
        send(zpair.at[1 - core], to, psem.at[8], qsem.at[8], here.sibling)
        to[...] = zpair[core]

    for _ in factor:
        pass
    rr = lax.broadcasted_iota(jnp.int32, (R, R), 0)
    cc = lax.broadcasted_iota(jnp.int32, (R, R), 1)
    inverse = jnp.where(cc <= rr, x_ref[...], 0.0)
    high = inverse.astype(BF)
    low = (inverse - high.astype(F32)).astype(BF)

    @pl.when(n < 7)
    def _():
        wait_bytes(zpair.at[0], qsem.at[8])
        pbuf[...] = (dot(high, zall[...]) + dot(low, zall[...])).astype(BF)
        for k in FAR_FIRST:
            send(pbuf.at[ds(((n + k) % NY) * 32, 32)], precv.at[n], psem.at[7], qsem.at[7], here.y_peer(k))
        precv[n] = pbuf[ds(n * 32, 32)]

    rows = yb[ds(core * H + n * 16, 16), :]
    basis_ref[...] = lax.dot_general(
        rows, inverse, (((1,), (1,)), ((), ())), preferred_element_type=F32, precision=lax.Precision.HIGHEST
    ) * math.sqrt(D)
    z.by_place(0, precv, qsem.at[7])

    for j in range(6):
        proj_ref[:, j * 128:(j + 1) * 128] = precv[j].astype(F32)
    proj_ref[:, 768:832] = precv[6][:, 0:64].astype(F32)

    @pl.when(n < 7)
    def _():
        wait_bytes(zpair.at[0], psem.at[8])
        wait_bytes(precv, psem.at[7])


def kernel(wt_hbm, u_hbm, s_hbm, basis_ref, proj_ref, *scratch):
    drains = []
    body(wt_hbm, u_hbm, s_hbm, basis_ref, proj_ref, scratch, drains)
    for drain in drains:
        drain()


def on_device(weight, whitening, sketch):
    vmem = pl.BlockSpec(memory_space=pltpu.VMEM)
    hbm = pl.BlockSpec(memory_space=pltpu.HBM)
    vm = pltpu.VMEM
    scratch = []
    for lay in WIDE:
        scratch += wide_scratch(lay)
    for width in NARROW:
        scratch += narrow_scratch(width)
    scratch += gram_scratch() + column_scratch() + column_scratch()
    scratch += [
        vm((2, 832, 1024), BF),
        vm((2 * H, 1024), BF),
        vm((832, R), BF),
        vm((H, 1024), BF),
        vm((H, 1024), BF),
        vm((H, 1024), F32),
        vm((H, 1024), BF),
        vm((H, 1024), BF),
        vm((H, 1024), BF),
        vm((H, 1024), BF),
        vm((H, 2 * H), BF),
        vm((2, H, 896), BF),
        vm((R, 2 * H), BF),
        vm((2 * H, R), F32),
        vm((R, R), F32),
        vm((2, H, 128), BF),
        vm((R, 128), BF),
        vm((R, 128), BF),
        vm((7, 32, 128), BF),
        pltpu.SemaphoreType.DMA((3,)),
        pltpu.SemaphoreType.DMA((NX,)),
        pltpu.SemaphoreType.DMA((NX,)),
        pltpu.SemaphoreType.DMA((9,)),
        pltpu.SemaphoreType.DMA((9,)),
    ]
    return pl.pallas_call(
        kernel,
        out_shape=(
            jax.ShapeDtypeStruct((16, R), F32),
            jax.ShapeDtypeStruct((32, 832), F32),
        ),
        in_specs=[hbm] * 3,
        out_specs=(vmem, vmem),
        scratch_shapes=scratch,
        compiler_params=pltpu.CompilerParams(
            collective_id=0, has_side_effects=True, vmem_limit_bytes=60 * 1024 * 1024
        ),
        cost_estimate=pl.CostEstimate(flops=2_300_000_000, bytes_accessed=3_000_000, transcendentals=256),
    )(weight.T, whitening, sketch)


def solution(mesh):
    placed = (P("narrow", "wide"), P("wide", "narrow"), P("wide", None))
    return jax.shard_map(
        on_device,
        mesh=mesh,
        in_specs=placed,
        out_specs=(P(("wide", "narrow"), None), P("narrow", "wide")),
        check_vma=False,
    )
```
